512 devices in a mesh: ctx: 128 (over z, y, core), ch: 4 (over x).
Axes of the slice: x: 4, y: 8, z: 8, core: 2. Of those that a mesh axis runs over, the one named last changes fastest.
Arguments:
- streams: bfloat16 [3, 16384, 4096], P(None, 'ctx', 'ch'), may hold values from -6 to 6
- seq_lengths: int32 [8], replicated, may hold values from 1 to 8192, 16384 in all
- conv_weight: float32 [3, 7, 4096], P(None, None, 'ch'), may hold values from -2.4 to 2.4
- rate: float32 [4096, 16], P('ch'), may hold values from 2e-05 to 0.25
- modal_gain: float32 [4096, 16], P('ch'), may hold values from -1.8 to 1.8
- cotangent: bfloat16 [16384, 4096], P('ctx', 'ch'), may hold values from -6 to 6
Outputs:
- output: bfloat16 [16384, 4096], P('ctx', 'ch')
- stream_grads: bfloat16 [3, 16384, 4096], P(None, 'ctx', 'ch')
- clipped_weight_grad: float32 [3, 7, 4096], P(None, None, 'ch')
The draws below stay inside these ranges and needn't reach their ends.
Inputs may be any that keep to these rules, and one draw needn't show every extreme that they name: `seq_lengths`: 8 sequences that fill the 16384 positions in order; the longest is exactly 8192.
All inputs are finite; a program needn't handle non-finite values.
Results may differ from the reference program's by a relative error of at most 0.0057.
Values may be sent and summed in bfloat16 or wider, within the bound.
No kernel may reach another device: no remote copies, remote signals or barrier semaphores. Data moves between devices by JAX's collectives and lax.ppermute only.
A program may use at most 128 MiB of HBM per device.

```python
import math
import jax
import jax.numpy as jnp
import numpy as np
from jax import lax

CH = 4096
MODES = 16
NSEQ = 8
TOKENS = 16384
SEQ_MOST = 8192


def block_levels(rng, dims, split, least, top_value):
    level = 1.0
    for dim, shards_of in split:
        steps = jax.random.uniform(jax.random.fold_in(jax.random.fold_in(rng, 6), dim), (shards_of,), jnp.float32, least / len(split), top_value / len(split))
        level = level * jnp.repeat(jnp.exp(steps), dims[dim] // shards_of).reshape((-1,) + (1,) * (len(dims) - 1 - dim))
    return level


def profile(number_of, total, reach, lean):
    loads = [(1 << 20) // math.isqrt(rank ** lean) + 1 for rank in range(2, number_of + 1)]
    surplus, counts = total - reach - (number_of - 1), [1] * (number_of - 1)
    while surplus > 0:
        movable = [i for i in range(number_of - 1) if counts[i] < reach]
        mass, left = sum([loads[i] for i in movable]), surplus
        for i in movable:
            extra = min(reach - counts[i], max(1, left * loads[i] // mass), surplus)
            counts[i] = counts[i] + extra
            surplus = surplus - extra
    return np.array([reach] + counts)


def uneven(rng, amount, total, most, skew):
    if amount == 2:
        one = jax.random.randint(rng, (), max(1, total - most), min(most, total - 1) + 1)
        return jnp.stack([one, total - one])
    sizes = jnp.asarray(profile(amount, total, most, skew), jnp.int32)
    twos = (amount - 1) // 2
    donor, receiver = sizes[1:1 + 2 * twos:2], sizes[2:2 + 2 * twos:2]
    slack = jnp.minimum(donor - 1, most - receiver)
    shifted = jax.random.randint(jax.random.fold_in(rng, 1), (twos,), 0, 1 << 20) % (slack + 1)
    sizes = sizes.at[1:1 + 2 * twos:2].set(donor - shifted).at[2:2 + 2 * twos:2].set(receiver + shifted)
    return sizes[jax.random.permutation(jax.random.fold_in(rng, 2), amount)]


def centred(stream_key, shape, scale, limit, split=(), kind=jnp.bfloat16):
    array = scale * jax.random.normal(stream_key, shape, jnp.float32)
    if split:
        array = array * block_levels(stream_key, shape, split, -0.22, 0.18)
    return jnp.clip(array, -limit, limit).astype(kind)


def setup_inputs(seed: int = 0) -> dict:
    arg_keys = jax.random.split(jax.random.key(seed), 7)
    streams = centred(arg_keys[0], (3, TOKENS, CH), 1.0, 6.0, ((1, 128), (2, 4)))
    seq_lengths = uneven(arg_keys[1], NSEQ, TOKENS, SEQ_MOST, 2).astype(jnp.int32)
    conv_weight = centred(arg_keys[2], (3, 7, CH), 0.4, 2.4, ((2, 4),), jnp.float32)
    rate = jnp.clip(jnp.exp(math.log(0.25) - 9.433484 * jax.random.uniform(arg_keys[3], (CH, MODES), jnp.float32) ** block_levels(arg_keys[3], (CH, MODES), ((0, 4),), -0.2, 0.2)), 1.9999999494757503e-05, 0.25)
    modal_gain = centred(arg_keys[4], (CH, MODES), 0.3, 1.8, ((0, 4),), jnp.float32)
    cotangent = centred(arg_keys[5], (TOKENS, CH), 1.0, 6.0, ((0, 128), (1, 4)))
    return dict(streams=streams, seq_lengths=seq_lengths, conv_weight=conv_weight, rate=rate, modal_gain=modal_gain, cotangent=cotangent)


def segment_info(seq_lengths, total):
    starts_at = jnp.cumsum(seq_lengths) - seq_lengths
    places = jnp.arange(total, dtype=jnp.int32)
    segment = lax.optimization_barrier(jnp.sum((starts_at[None, :] <= places[:, None]).astype(jnp.int32), axis=1))
    opens = jnp.any(starts_at[None, :] == places[:, None], axis=1)
    return (segment, opens)

def shift_down(values, fill, steps):
    if steps == 0:
        return values
    head = jnp.full((steps,) + values.shape[1:], fill, values.dtype)
    return jnp.concatenate([head, values[:values.shape[0] - steps]], axis=0)

def shift_up(values, fill, steps):
    if steps == 0:
        return values
    trailing_rows = jnp.full((steps,) + values.shape[1:], fill, values.dtype)
    return jnp.concatenate([values[steps:], trailing_rows], axis=0)

def short_filter(values, weights, segment):
    result = jnp.zeros(values.shape, jnp.float32)
    for j in range(7):
        moved = shift_down(values, 0.0, j)
        same = (segment == shift_down(segment, -1, j)).astype(jnp.float32)
        result = result + weights[j][None, :] * moved * same[:, None]
    return result

def short_adjoint(grads, weights, segment):
    result = jnp.zeros(grads.shape, jnp.float32)
    for j in range(7):
        moved = shift_up(grads, 0.0, j)
        same = (segment == shift_up(segment, -1, j)).astype(jnp.float32)
        result = result + weights[j][None, :] * moved * same[:, None]
    return result

def short_weight_grad(grads, values, segment):
    rows = []
    for j in range(7):
        moved = shift_down(values, 0.0, j)
        same = (segment == shift_down(segment, -1, j)).astype(jnp.float32)
        rows.append(lax.optimization_barrier(jnp.sum(grads * moved * same[:, None], axis=0)))
    return jnp.stack(rows, axis=0)

def modal_scan(values, resets, decay, coef, backwards):

    def advance(state, item):
        row, reset = item
        state = jnp.where(reset, jnp.float32(0.0), decay * state) + row[:, None]
        return (state, lax.optimization_barrier(jnp.sum(coef * state, axis=1)))
    init = jnp.zeros(decay.shape, jnp.float32)
    _, outs = lax.scan(advance, init, (values, resets), reverse=backwards)
    return outs

def reference(streams, seq_lengths, conv_weight, rate, modal_gain, cotangent):
    total = streams.shape[1]
    segment, opens = segment_info(seq_lengths, total)
    closes = jnp.concatenate([opens[1:], jnp.ones((1,), dtype=bool)])
    inputs = streams.astype(jnp.float32)
    qc = short_filter(inputs[0], conv_weight[0], segment)
    kc = short_filter(inputs[1], conv_weight[1], segment)
    vc = short_filter(inputs[2], conv_weight[2], segment)
    decay = jnp.exp(-rate)
    coef = modal_gain * jnp.sqrt(-jnp.expm1(-2.0 * rate))
    gated = (kc * vc).astype(jnp.bfloat16)
    long_out = modal_scan(gated.astype(jnp.float32), opens, decay, coef, False).astype(jnp.bfloat16)
    long_float = long_out.astype(jnp.float32)
    output = (qc * long_float).astype(jnp.bfloat16)
    upstream = cotangent.astype(jnp.float32)
    grad_long = (upstream * qc).astype(jnp.bfloat16)
    grad_gated = modal_scan(grad_long.astype(jnp.float32), closes, decay, coef, True).astype(jnp.bfloat16)
    grad_float = grad_gated.astype(jnp.float32)
    filtered_grads = [upstream * long_float, grad_float * vc, grad_float * kc]
    stream_grads = jnp.stack([short_adjoint(filtered_grads[i], conv_weight[i], segment) for i in range(3)], axis=0).astype(jnp.bfloat16)
    weight_grad = jnp.stack([short_weight_grad(filtered_grads[i], inputs[i], segment) for i in range(3)], axis=0)
    squares = jnp.sum(weight_grad * weight_grad)
    factor = jnp.minimum(jnp.float32(1.0), 1.0 / jnp.sqrt(squares + 1e-06))
    return (output, stream_grads, weight_grad * factor)
```

```python
import functools

import jax
import jax.numpy as jnp
from jax import lax
from jax.experimental import pallas as pl
from jax.experimental.pallas import tpu as pltpu
from jax.sharding import PartitionSpec as P

F32 = jnp.float32
BF16 = jnp.bfloat16
TAPS = 7
REACH = TAPS - 1
TOK = 128
LANES = 128
OWN = 8
SUB = 8

LEFT = LANES - 3 * REACH
RIGHT = 0
STATE = 18
MODES = 16
GRADS = STATE + 4 * MODES


def rounded(value):
    return value.astype(BF16).astype(F32)


def halves(value):
    high = value.astype(BF16)
    return high, (value - high.astype(F32)).astype(BF16)


def one_minus_exp(x):
    series = jnp.full_like(x, 1.0)
    for n in range(11, 1, -1):
        series = 1.0 - (x * F32(1.0 / n)) * series
    return x * series


def gains(rate, gain):
    return gain * jnp.sqrt(one_minus_exp(2.0 * rate))


def start_list(seq_ref):
    starts = [jnp.int32(0)]
    for n in range(seq_ref.shape[0]):
        starts.append(starts[-1] + seq_ref[n])
    return starts


def dot(a, b):
    return lax.dot_general(a, b, (((1,), (0,)), ((), ())), preferred_element_type=F32)


def dot_t(a, b):
    return lax.dot_general(a, b, (((1,), (1,)), ((), ())), preferred_element_type=F32)


def turn_kernel(streams, cotangent, out):
    for pair in range(2):
        for k in range(SUB):
            cols = pl.ds(k * LANES, LANES)
            first = streams[2 * pair, :, cols]
            second = streams[1, :, cols] if pair == 0 else cotangent[:, cols]
            a = first.astype(F32).T.reshape(LANES // OWN, OWN, TOK)
            b = second.astype(F32).T.reshape(LANES // OWN, OWN, TOK)
            out[pl.ds(k * (LANES // OWN), LANES // OWN), pl.ds(pair * 16, 16), :] = (
                jnp.concatenate([a, b], axis=1).astype(BF16)
            )


ROWS_OF = (0, 8, 16, 24)


def owner_kernel(
    total, seq, moved, weight, rate, gain, out, sh, wide, u, dz, kc, vc, zs, ds, pay, fixf, fixb, prm
):
    blocks = moved.shape[0]
    index = lax.axis_index("ctx")
    starts = start_list(seq)
    starts[-1] = jnp.int32(total)
    nseq = seq.shape[0]
    lane = lax.broadcasted_iota(jnp.int32, (SUB, LANES), 1)

    chunk = pl.multiple_of((index // (LANES // OWN)) * LANES, LANES)
    back = lax.rem(LANES - lax.rem(index, LANES // OWN) * OWN, LANES)
    cols = pl.ds(chunk, LANES)
    prm[...] = jnp.zeros_like(prm)
    prm[0:MODES, :] = pltpu.roll(rate[:, cols], back, 1)
    prm[MODES : 2 * MODES, :] = pltpu.roll(gain[:, cols], back, 1)
    for i in range(3):
        prm[32 + 8 * i : 32 + 8 * i + TAPS, :] = weight[i, :, cols]
    prm[32:56, :] = pltpu.roll(prm[32:56, :], back, 1)
    own = prm[...].T[0:OWN, :]
    for i in range(3):
        for j in range(TAPS):
            f = 32 + 8 * i + j
            wide[i * TAPS + j] = jnp.broadcast_to(own[:, f : f + 1], (SUB, LANES))
    rate_rows = jnp.concatenate(
        [jnp.broadcast_to(own[:, m : m + 1], (SUB, LANES)) for m in range(MODES)], axis=0
    )
    gain_rows = jnp.concatenate(
        [
            jnp.broadcast_to(own[:, MODES + m : MODES + m + 1], (SUB, LANES))
            for m in range(MODES)
        ],
        axis=0,
    )
    coef_rows = gains(rate_rows, gain_rows)

    def filtering(b, masked):
        now = moved[b].astype(F32)
        before = moved[jnp.maximum(b - 1, 0)].astype(F32)
        if masked:
            place = b * TOK + lane
            since = jnp.zeros((SUB, LANES), jnp.int32)
            for s in starts[:-1]:
                since = jnp.where(s <= place, s, since)
            since = place - since
        done = []
        for i in range(3):
            x = now[ROWS_OF[i] : ROWS_OF[i] + 8]
            p = before[ROWS_OF[i] : ROWS_OF[i] + 8]
            acc = wide[i * TAPS] * x
            for j in range(1, TAPS):
                moved_x = pltpu.roll(jnp.where(lane >= LANES - j, p, x), j, 1)
                if masked:
                    moved_x = jnp.where(since >= j, moved_x, 0.0)
                sh[i * REACH + j - 1, b] = moved_x
                acc = acc + wide[i * TAPS + j] * moved_x
            done.append(acc)
        rows = pl.ds(pl.multiple_of(b * SUB, SUB), SUB)
        u[rows, :] = rounded(done[1] * done[2])
        dz[rows, :] = rounded(now[24:32] * done[0])
        kc[rows, :] = done[1]
        vc[rows, :] = done[2]

    def filter_loop(b, _):
        filtering(b, False)
        return 0

    lax.fori_loop(0, blocks, filter_loop, 0, unroll=2)
    for s in starts[:-1]:
        b = s // TOK
        filtering(b, True)
        filtering(jnp.minimum(b + 1, blocks - 1), True)

    for n in range(nseq):
        b = starts[n] // TOK
        rows = pl.ds(pl.multiple_of(b * SUB, SUB), SUB)
        place = b * TOK + lane
        fixf[n * SUB : (n + 1) * SUB, :] = jnp.where(place >= starts[n], u[rows, :], 0.0)
        fixb[n * SUB : (n + 1) * SUB, :] = jnp.where(place < starts[n], dz[rows, :], 0.0)

    row = lax.broadcasted_iota(jnp.int32, (blocks, TOK), 0)
    col = lax.broadcasted_iota(jnp.int32, (blocks, TOK), 1)
    head = jnp.ones((blocks, TOK), F32)
    tail = jnp.ones((blocks, TOK), F32)
    for s in starts[:-1]:
        here = row == s // TOK
        head = jnp.where(here & (col >= lax.rem(s, TOK)), 0.0, head)
        tail = jnp.where(here & (col < lax.rem(s, TOK)), 0.0, tail)

    lag = lax.broadcasted_iota(jnp.int32, (LANES, LANES), 1).astype(F32)
    ending = halves(jnp.exp(-rate_rows * (TOK - 1.0 - lag)))
    opening = halves(jnp.exp(-rate_rows * lag))
    lead_f = halves(coef_rows * jnp.exp(-rate_rows * (lag + 1.0)))
    lead_b = halves(coef_rows * jnp.exp(-rate_rows * (TOK - lag)))
    whole = jnp.exp(-rate_rows * TOK).T[0:1, :]
    taps = (coef_rows * jnp.exp(-rate_rows * lag)).reshape(MODES, OWN, LANES).sum(axis=0)

    mine = lax.rem(lax.broadcasted_iota(jnp.int32, (blocks, LANES), 1), OWN)
    end_f = jnp.zeros((blocks, LANES), F32)
    end_b = jnp.zeros((blocks, LANES), F32)
    for c in range(OWN):
        uc = (u[pl.ds(c, blocks, stride=OWN), :] * tail).astype(BF16)
        dc = (dz[pl.ds(c, blocks, stride=OWN), :] * head).astype(BF16)
        ef = dot_t(uc, ending[0]) + dot_t(uc, ending[1])
        eb = dot_t(dc, opening[0]) + dot_t(dc, opening[1])
        end_f = jnp.where(mine == c, ef, end_f)
        end_b = jnp.where(mine == c, eb, end_b)

    keep_f = head[:, TOK - 1 : TOK] * whole
    keep_b = keep_f
    step = 1
    while step < blocks:
        low = row >= step
        end_f = end_f + jnp.where(low, keep_f * pltpu.roll(end_f, step, 0), 0.0)
        keep_f = jnp.where(low, keep_f * pltpu.roll(keep_f, step, 0), 0.0)
        high = row < blocks - step
        end_b = end_b + jnp.where(high, keep_b * pltpu.roll(end_b, blocks - step, 0), 0.0)
        keep_b = jnp.where(high, keep_b * pltpu.roll(keep_b, blocks - step, 0), 0.0)
        step *= 2
    state_f = jnp.where(row >= 1, pltpu.roll(end_f, 1, 0), 0.0)
    state_b = jnp.where(row < blocks - 1, pltpu.roll(end_b, blocks - 1, 0), 0.0)
    sf = halves(state_f)
    sb = halves(state_b)

    pick_row = lax.broadcasted_iota(jnp.int32, (LANES, LANES), 0)
    pick_col = lax.broadcasted_iota(jnp.int32, (LANES, LANES), 1)
    zero = jnp.zeros((blocks, LANES), BF16)
    for c in range(OWN):
        strip = jnp.broadcast_to(taps[c : c + 1, :], (LANES, LANES))
        strip = pltpu.roll(strip, 0, 1, stride=1, stride_axis=0)
        kern = halves(jnp.where(pick_col >= pick_row, strip, 0.0))
        of_c = mine == c
        uc = jnp.concatenate(
            [u[pl.ds(c, blocks, stride=OWN), :], fixf[pl.ds(c, nseq, stride=OWN), :]], axis=0
        ).astype(BF16)
        dc = jnp.concatenate(
            [dz[pl.ds(c, blocks, stride=OWN), :], fixb[pl.ds(c, nseq, stride=OWN), :]], axis=0
        ).astype(BF16)
        zc = dot(uc, kern[0]) + dot(uc, kern[1])
        rc = dot_t(dc, kern[0]) + dot_t(dc, kern[1])
        fixf[pl.ds(c, nseq, stride=OWN), :] = zc[blocks:]
        fixb[pl.ds(c, nseq, stride=OWN), :] = rc[blocks:]
        fh, fl = [jnp.where(of_c, x, zero) for x in sf]
        bh, bl = [jnp.where(of_c, x, zero) for x in sb]
        carry_f = dot(fh, lead_f[0]) + dot(fh, lead_f[1]) + dot(fl, lead_f[0])
        carry_b = dot(bh, lead_b[0]) + dot(bh, lead_b[1]) + dot(bl, lead_b[0])
        zs[pl.ds(c, blocks, stride=OWN), :] = zc[:blocks] + head * carry_f
        ds[pl.ds(c, blocks, stride=OWN), :] = rc[:blocks] + tail * carry_b
        spread = jnp.zeros((blocks, LANES), F32)
        for g, part in enumerate((fh, fl, bh, bl)):
            goes = (lax.rem(pick_row, OWN) == c) & (
                pick_col == STATE + g * MODES + pick_row // OWN
            )
            spread = spread + dot(part, jnp.where(goes, 1.0, 0.0).astype(BF16))
        pay[pl.ds(c, blocks, stride=OWN), :] = spread
    for n in range(nseq):
        b = starts[n] // TOK
        rows = pl.ds(pl.multiple_of(b * SUB, SUB), SUB)
        place = b * TOK + lane
        fresh = (place >= starts[n]) & (place < starts[n + 1])
        zs[rows, :] = jnp.where(fresh, fixf[n * SUB : (n + 1) * SUB, :], zs[rows, :])
        if n > 0:
            fresh = (place >= starts[n - 1]) & (place < starts[n])
            ds[rows, :] = jnp.where(fresh, fixb[n * SUB : (n + 1) * SUB, :], ds[rows, :])

    def gradient(b, acc):
        rows = pl.ds(pl.multiple_of(b * SUB, SUB), SUB)
        now = moved[b].astype(F32)
        z = rounded(zs[rows, :])
        d = rounded(ds[rows, :])
        df = (now[24:32] * z, d * vc[rows, :], d * kc[rows, :])
        new = []
        for i in range(3):
            new.append(acc[i * TAPS] + df[i] * now[ROWS_OF[i] : ROWS_OF[i] + 8])
            for j in range(1, TAPS):
                new.append(acc[i * TAPS + j] + df[i] * sh[i * REACH + j - 1, b])
        halo = jnp.where(lane < REACH, df[0], 0.0)
        for i in (1, 2):
            part = pltpu.roll(df[i], i * REACH, 1)
            halo = jnp.where((lane >= i * REACH) & (lane < (i + 1) * REACH), part, halo)
        target = pl.ds(pl.multiple_of(jnp.maximum(b - 1, 0) * SUB, SUB), SUB)
        pay[target, :] = pay[target, :] + jnp.where(b > 0, halo, 0.0)
        return tuple(new)

    acc = lax.fori_loop(
        0, blocks, gradient, tuple(jnp.zeros((SUB, LANES), F32) for _ in range(3 * TAPS))
    )
    grads = jnp.zeros((SUB, LANES), F32)
    for f in range(3 * TAPS):
        grads = jnp.where(lane == GRADS + f, jnp.sum(acc[f], axis=1, keepdims=True), grads)

    def finish(p, _):
        tiles = []
        for b in (2 * p, 2 * p + 1):
            before = moved[jnp.maximum(b - 1, 0)].astype(F32)
            value = pay[pl.ds(pl.multiple_of(b * SUB, SUB), SUB), :] + grads
            for i in range(3):
                x = before[ROWS_OF[i] : ROWS_OF[i] + 8]
                first = LEFT + i * REACH
                x = x if i == 2 else pltpu.roll(x, first - (TOK - REACH) + LANES, 1)
                value = jnp.where((lane >= first) & (lane < first + REACH), x, value)
            tiles.append(value)
        out[pl.ds(pl.multiple_of(p * 16, 16), 16), :] = jnp.concatenate(tiles, axis=0).astype(BF16)
        return 0

    lax.fori_loop(0, blocks // 2, finish, 0)


def shard_kernel(
    total,
    seq,
    streams,
    cotangent,
    fields,
    weight,
    rate,
    gain,
    out,
    grads_out,
    wgrad,
    squares,
    xs,
    cots,
    fs,
    ws,
    prm,
    kcs,
    vcs,
    dzs,
    dfs,
    outs,
    sgs,
):
    index = lax.axis_index("ctx")
    local = [s - index * TOK for s in start_list(seq)]
    local[-1] = total - index * TOK

    for k in range(SUB):
        cols = pl.ds(k * LANES, LANES)
        turned = fields[pl.ds(k * LANES, LANES), :].astype(F32).T
        for g in range(LANES // 8):
            fs[pl.ds(g * 64 + k, 8, stride=SUB), :] = turned[g * 8 : g * 8 + 8]
        for g in range(MODES // 8):
            r = rate[g * 8 : g * 8 + 8, cols]
            prm[pl.ds(g * 64 + k, 8, stride=SUB), :] = jnp.exp(-r)
            prm[pl.ds(MODES * SUB + g * 64 + k, 8, stride=SUB), :] = gains(
                r, gain[g * 8 : g * 8 + 8, cols]
            )
        for i in range(3):
            ws[pl.ds(i * 64 + k, TAPS, stride=SUB), :] = weight[i, :, cols]
        for g in range(TOK // 16):
            for i in range(4):
                x = streams[i, pl.ds(g * 16, 16), cols] if i < 3 else cotangent[pl.ds(g * 16, 16), cols]
                x = x.astype(F32)
                for h in range(2):
                    t = g * 16 + h * 8
                    if i < 3:
                        xs[i, pl.ds((t + REACH) * SUB + k, 8, stride=SUB), :] = x[h * 8 : h * 8 + 8]
                    else:
                        cots[pl.ds(t * SUB + k, 8, stride=SUB), :] = x[h * 8 : h * 8 + 8]
    for i in range(3):
        xs[i, 0 : REACH * SUB, :] = fs[(LEFT + i * REACH) * SUB : (LEFT + (i + 1) * REACH) * SUB, :]
        dfs[i, TOK * SUB : (TOK + REACH) * SUB, :] = fs[
            (RIGHT + i * REACH) * SUB : (RIGHT + (i + 1) * REACH) * SUB, :
        ]

    def tile(ref, n):
        return ref[pl.ds(n * SUB, SUB), :]

    def at(ref, t):
        return ref[pl.ds(pl.multiple_of(t * SUB, SUB), SUB), :]

    def at3(ref, i, t):
        return ref[i, pl.ds(pl.multiple_of(t * SUB, SUB), SUB), :]

    def put(ref, t, value):
        ref[pl.ds(pl.multiple_of(t * SUB, SUB), SUB), :] = value

    def put3(ref, i, t, value):
        ref[i, pl.ds(pl.multiple_of(t * SUB, SUB), SUB), :] = value

    def since(t):
        last = local[0]
        for s in local[1:]:
            last = jnp.where(s <= t, s, last)
        return t - last

    def until(t):
        following = local[-1]
        for s in local[-2::-1]:
            following = jnp.where(s > t, s, following)
        return following - t

    def near(t0):
        found = jnp.bool_(False)
        for s in local:
            found = found | ((s >= t0 - REACH) & (s < t0 + 8 + REACH + 1))
        return found

    def forward(t0, state, masked):
        ages = [since(t0 + r) for r in range(8)] if masked else None
        done = []
        for i in range(3):
            w = [tile(ws, i * 8 + j) for j in range(TAPS)]
            x = [at3(xs, i, t0 + n) for n in range(8 + REACH)]
            row = []
            for r in range(8):
                acc = w[0] * x[r + REACH]
                for j in range(1, TAPS):
                    term = w[j] * x[r + REACH - j]
                    if masked:
                        term = jnp.where(ages[r] >= j, term, 0.0)
                    acc = acc + term
                row.append(acc)
            done.append(row)
        state = list(state)
        for r in range(8):
            t = t0 + r
            q, k, v = done[0][r], done[1][r], done[2][r]
            put(kcs, t, k)
            put(vcs, t, v)
            c = at(cots, t)
            put(dzs, t, rounded(c * q))
            u = rounded(k * v)
            z = jnp.zeros((SUB, LANES), F32)
            for m in range(MODES):
                old = state[m]
                if masked:
                    old = jnp.where(ages[r] > 0, old, 0.0)
                state[m] = tile(prm, m) * old + u
                z = z + tile(prm, MODES + m) * state[m]
            z = rounded(z)
            put(outs, t, q * z)
            put3(dfs, 0, t, c * z)
        return tuple(state)

    def backward(t0, state, masked):
        gaps = [until(t0 + r) for r in range(8)] if masked else None
        state = list(state)
        for r in range(7, -1, -1):
            t = t0 + r
            g = at(dzs, t)
            d = jnp.zeros((SUB, LANES), F32)
            for m in range(MODES):
                old = state[m]
                if masked:
                    old = jnp.where(gaps[r] > 1, old, 0.0)
                state[m] = tile(prm, m) * old + g
                d = d + tile(prm, MODES + m) * state[m]
            d = rounded(d)
            put3(dfs, 1, t, d * at(vcs, t))
            put3(dfs, 2, t, d * at(kcs, t))
        for i in range(3):
            w = [tile(ws, i * 8 + j) for j in range(TAPS)]
            y = [at3(dfs, i, t0 + n) for n in range(8 + REACH)]
            for r in range(8):
                acc = w[0] * y[r]
                for j in range(1, TAPS):
                    term = w[j] * y[r + j]
                    if masked:
                        term = jnp.where(gaps[r] > j, term, 0.0)
                    acc = acc + term
                put3(sgs, i, t0 + r, acc)
        return tuple(state)

    def entering(g):
        return tuple(
            tile(fs, STATE + g * MODES + m) + tile(fs, STATE + (g + 1) * MODES + m)
            for m in range(MODES)
        )

    def step_f(n, state):
        t0 = n * 8
        return lax.cond(
            near(t0),
            lambda s: forward(t0, s, True),
            lambda s: forward(t0, s, False),
            state,
        )

    def step_b(n, state):
        t0 = TOK - 8 - n * 8
        return lax.cond(
            near(t0),
            lambda s: backward(t0, s, True),
            lambda s: backward(t0, s, False),
            state,
        )

    lax.fori_loop(0, TOK // 8, step_f, entering(0))
    lax.fori_loop(0, TOK // 8, step_b, entering(2))

    total_sq = jnp.zeros((SUB, LANES), F32)
    for f in range(3 * TAPS):
        g = tile(fs, GRADS + f)
        total_sq = total_sq + g * g
    squares[...] = jnp.broadcast_to(jnp.sum(total_sq), (1, LANES))
    for k in range(SUB):
        cols = pl.ds(k * LANES, LANES)
        for i in range(3):
            wgrad[i, :, cols] = fs[pl.ds((GRADS + i * TAPS) * SUB + k, TAPS, stride=SUB), :]
        for g in range(TOK // 16):
            for i in range(4):
                parts = []
                for h in range(2):
                    rows = pl.ds((g * 16 + h * 8) * SUB + k, 8, stride=SUB)
                    parts.append(sgs[i, rows, :] if i < 3 else outs[rows, :])
                both = jnp.concatenate(parts, axis=0).astype(BF16)
                if i < 3:
                    grads_out[i, pl.ds(g * 16, 16), cols] = both
                else:
                    out[pl.ds(g * 16, 16), cols] = both


def vmem():
    return pl.BlockSpec(memory_space=pltpu.VMEM)


def smem():
    return pl.BlockSpec(memory_space=pltpu.SMEM)


def body(streams, seq_lengths, conv_weight, rate, modal_gain, cotangent):
    tok, chans = streams.shape[1:]
    shards = lax.axis_size("ctx")
    total = tok * shards
    rate_t, gain_t = rate.T, modal_gain.T
    params = pltpu.CompilerParams(vmem_limit_bytes=48 * 1024 * 1024)
    turned = pl.pallas_call(
        turn_kernel,
        out_shape=jax.ShapeDtypeStruct((shards, 4 * OWN, tok), BF16),
        in_specs=[vmem()] * 2,
        out_specs=vmem(),
        compiler_params=params,
        name="turn",
    )(streams, cotangent)
    moved = lax.all_to_all(turned, "ctx", split_axis=0, concat_axis=0, tiled=True)
    rows = shards * OWN
    plane = pltpu.VMEM((rows, LANES), F32)
    payload = pl.pallas_call(
        functools.partial(owner_kernel, total),
        out_shape=jax.ShapeDtypeStruct((rows, LANES), BF16),
        in_specs=[smem()] + [vmem()] * 4,
        out_specs=vmem(),
        scratch_shapes=[
            pltpu.VMEM((3 * REACH, shards, SUB, LANES), F32),
            pltpu.VMEM((3 * TAPS, SUB, LANES), F32),
        ]
        + [plane] * 7
        + [pltpu.VMEM((8 * SUB, LANES), F32)] * 2
        + [pltpu.VMEM((LANES, LANES), F32)],
        compiler_params=params,
        name="owner",
    )(seq_lengths, moved, conv_weight, rate_t, gain_t)
    fields = lax.all_to_all(
        payload.reshape(shards, OWN, LANES), "ctx", split_axis=0, concat_axis=0, tiled=True
    ).reshape(rows, LANES)
    plane = pltpu.VMEM((tok * SUB, LANES), F32)
    tall = pltpu.VMEM((3, (tok + REACH) * SUB, LANES), F32)
    output, stream_grads, weight_grad, squares = pl.pallas_call(
        functools.partial(shard_kernel, total),
        out_shape=[
            jax.ShapeDtypeStruct((tok, chans), BF16),
            jax.ShapeDtypeStruct((3, tok, chans), BF16),
            jax.ShapeDtypeStruct((3, TAPS, chans), F32),
            jax.ShapeDtypeStruct((1, LANES), F32),
        ],
        in_specs=[smem()] + [vmem()] * 6,
        out_specs=[vmem()] * 4,
        scratch_shapes=[
            tall,
            plane,
            pltpu.VMEM((LANES * SUB, LANES), F32),
            pltpu.VMEM((3 * 8 * SUB, LANES), F32),
            pltpu.VMEM((2 * MODES * SUB, LANES), F32),
            plane,
            plane,
            plane,
            tall,
            plane,
            pltpu.VMEM((3, tok * SUB, LANES), F32),
        ],
        compiler_params=params,
        name="shard",
    )(seq_lengths, streams, cotangent, fields, conv_weight, rate_t, gain_t)
    squares = lax.psum(squares[0, 0], "ch")
    factor = jnp.minimum(jnp.float32(1.0), 1.0 / jnp.sqrt(squares + 1e-06))
    return output, stream_grads, weight_grad * factor


def solution(mesh):
    return jax.shard_map(
        body,
        mesh=mesh,
        in_specs=(
            P(None, "ctx", "ch"),
            P(),
            P(None, None, "ch"),
            P("ch", None),
            P("ch", None),
            P("ctx", "ch"),
        ),
        out_specs=(P("ctx", "ch"), P(None, "ctx", "ch"), P(None, None, "ch")),
        check_vma=False,
    )
```

```python
import functools

import jax
import jax.numpy as jnp
from jax import lax
from jax.experimental import pallas as pl
from jax.experimental.pallas import tpu as pltpu
from jax.sharding import PartitionSpec as P

F32 = jnp.float32
BF16 = jnp.bfloat16
TAPS = 7
REACH = TAPS - 1
TOK = 128
LANES = 128
OWN = 8
SUB = 8
GROUP = 8
STAGE = 99

LEFT = LANES - 3 * REACH
RIGHT = 0
STATE = 18
MODES = 16
GRADS = STATE + 4 * MODES


def rounded(value):
    return value.astype(BF16).astype(F32)


def halves(value):
    high = value.astype(BF16)
    return high, (value - high.astype(F32)).astype(BF16)


def one_minus_exp(x):
    series = jnp.full_like(x, 1.0)
    for n in range(11, 1, -1):
        series = 1.0 - (x * F32(1.0 / n)) * series
    return x * series


def gains(rate, gain):
    return gain * jnp.sqrt(one_minus_exp(2.0 * rate))


def start_list(seq_ref):
    starts = [jnp.int32(0)]
    for n in range(seq_ref.shape[0]):
        starts.append(starts[-1] + seq_ref[n])
    return starts


def dot(a, b):
    return lax.dot_general(a, b, (((1,), (0,)), ((), ())), preferred_element_type=F32)


def dot_t(a, b):
    return lax.dot_general(a, b, (((1,), (1,)), ((), ())), preferred_element_type=F32)


def turn_kernel(streams, cotangent, out):
    for pair in range(2):
        for k in range(SUB):
            cols = pl.ds(k * LANES, LANES)
            first = streams[2 * pair, :, cols]
            second = streams[1, :, cols] if pair == 0 else cotangent[:, cols]
            a = first.astype(F32).T.reshape(LANES // OWN, OWN, TOK)
            b = second.astype(F32).T.reshape(LANES // OWN, OWN, TOK)
            out[pl.ds(k * (LANES // OWN), LANES // OWN), pl.ds(pair * 16, 16), :] = (
                jnp.concatenate([a, b], axis=1).astype(BF16)
            )


ROWS_OF = (0, 8, 16, 24)


def owner_kernel(
    total, seq, moved, weight, rate, gain, out, sh, wide, u, dz, kc, vc, zs, ds, pay, halos, fixf, fixb, prm
):
    blocks = moved.shape[0]
    index = lax.axis_index("ctx")
    starts = start_list(seq)
    starts[-1] = jnp.int32(total)
    nseq = seq.shape[0]
    lane = lax.broadcasted_iota(jnp.int32, (SUB, LANES), 1)

    chunk = pl.multiple_of((index // (LANES // OWN)) * LANES, LANES)
    back = lax.rem(LANES - lax.rem(index, LANES // OWN) * OWN, LANES)
    cols = pl.ds(chunk, LANES)
    prm[...] = jnp.zeros_like(prm)
    prm[0:MODES, :] = pltpu.roll(rate[:, cols], back, 1)
    prm[MODES : 2 * MODES, :] = pltpu.roll(gain[:, cols], back, 1)
    for i in range(3):
        prm[32 + 8 * i : 32 + 8 * i + TAPS, :] = weight[i, :, cols]
    prm[32:56, :] = pltpu.roll(prm[32:56, :], back, 1)
    own = prm[...].T[0:OWN, :]
    for i in range(3):
        for j in range(TAPS):
            f = 32 + 8 * i + j
            wide[i * TAPS + j] = jnp.broadcast_to(own[:, f : f + 1], (SUB, LANES))
    rate_rows = jnp.concatenate(
        [jnp.broadcast_to(own[:, m : m + 1], (SUB, LANES)) for m in range(MODES)], axis=0
    )
    gain_rows = jnp.concatenate(
        [
            jnp.broadcast_to(own[:, MODES + m : MODES + m + 1], (SUB, LANES))
            for m in range(MODES)
        ],
        axis=0,
    )
    coef_rows = gains(rate_rows, gain_rows)

    def filtering(b, now, before, since):
        done = []
        for i in range(3):
            x = now[ROWS_OF[i] : ROWS_OF[i] + 8]
            p = before[ROWS_OF[i] : ROWS_OF[i] + 8]
            acc = wide[i * TAPS] * x
            for j in range(1, TAPS):
                moved_x = pltpu.roll(jnp.where(lane >= LANES - j, p, x), j, 1)
                if since is not None:
                    moved_x = jnp.where(since >= j, moved_x, 0.0)
                sh[i * REACH + j - 1, b] = moved_x
                acc = acc + wide[i * TAPS + j] * moved_x
            done.append(acc)
        rows = pl.ds(pl.multiple_of(b * SUB, SUB), SUB)
        u[rows, :] = rounded(done[1] * done[2])
        dz[rows, :] = rounded(now[24:32] * done[0])
        kc[rows, :] = done[1]
        vc[rows, :] = done[2]

    def filter_group(n, _):
        b0 = n * GROUP
        held = [moved[jnp.maximum(b0 - 1, 0)].astype(F32)]
        held += [moved[b0 + g].astype(F32) for g in range(GROUP)]
        for g in range(GROUP):
            filtering(b0 + g, held[g + 1], held[g], None)
        return 0

    lax.fori_loop(0, blocks // GROUP, filter_group, 0)
    if STAGE < 2:
        return
    for s in starts[:-1]:
        for near in (0, 1):
            b = jnp.minimum(s // TOK + near, blocks - 1)
            place = b * TOK + lane
            since = jnp.zeros((SUB, LANES), jnp.int32)
            for other in starts[:-1]:
                since = jnp.where(other <= place, other, since)
            filtering(
                b,
                moved[b].astype(F32),
                moved[jnp.maximum(b - 1, 0)].astype(F32),
                place - since,
            )

    for n in range(nseq):
        b = starts[n] // TOK
        rows = pl.ds(pl.multiple_of(b * SUB, SUB), SUB)
        place = b * TOK + lane
        fixf[n * SUB : (n + 1) * SUB, :] = jnp.where(place >= starts[n], u[rows, :], 0.0)
        fixb[n * SUB : (n + 1) * SUB, :] = jnp.where(place < starts[n], dz[rows, :], 0.0)
    if STAGE < 3:
        return

    row = lax.broadcasted_iota(jnp.int32, (blocks, TOK), 0)
    col = lax.broadcasted_iota(jnp.int32, (blocks, TOK), 1)
    head = jnp.ones((blocks, TOK), F32)
    tail = jnp.ones((blocks, TOK), F32)
    spot = row * TOK + col
    for s in starts[:-1]:
        base = s - lax.rem(s, TOK)
        head = jnp.where((spot >= s) & (spot < base + TOK), 0.0, head)
        tail = jnp.where((spot < s) & (spot >= base), 0.0, tail)

    lag = col.astype(F32)
    ending = halves(jnp.exp(-rate_rows * (TOK - 1.0 - lag)))
    falling = jnp.exp(-rate_rows * lag)
    opening = halves(falling)
    lead_f = halves(coef_rows * jnp.exp(-rate_rows * (lag + 1.0)))
    lead_b = halves(coef_rows * jnp.exp(-rate_rows * (TOK - lag)))
    whole = jnp.exp(-rate_rows * TOK).T[0:1, :]
    taps = (coef_rows * falling).reshape(MODES, OWN, LANES).sum(axis=0)

    mine = lax.rem(col, OWN)
    ending = jnp.concatenate(ending, axis=1)
    opening = jnp.concatenate(opening, axis=1)
    end_f = jnp.zeros((blocks, LANES), F32)
    end_b = jnp.zeros((blocks, LANES), F32)
    if STAGE < 4:
        zs[0:LANES, :] = head + tail + whole + lead_f[0].astype(F32) + lead_b[0].astype(F32)
        zs[0:LANES, :] = ending[:, :LANES].astype(F32) + opening[:, :LANES].astype(F32)
        zs[0:8, :] = taps
        return
    for c in range(OWN):
        uc = (u[pl.ds(c, blocks, stride=OWN), :] * tail).astype(BF16)
        dc = (dz[pl.ds(c, blocks, stride=OWN), :] * head).astype(BF16)
        ef = dot_t(jnp.concatenate([uc, uc], axis=1), ending)
        eb = dot_t(jnp.concatenate([dc, dc], axis=1), opening)
        end_f = jnp.where(mine == c, ef, end_f)
        end_b = jnp.where(mine == c, eb, end_b)
    if STAGE < 5:
        zs[0:LANES, :] = end_f + end_b
        return

    keep_f = head[:, TOK - 1 : TOK] * whole
    keep_b = keep_f
    step = 1
    while step < blocks:
        low = row >= step
        end_f = end_f + jnp.where(low, keep_f * pltpu.roll(end_f, step, 0), 0.0)
        keep_f = jnp.where(low, keep_f * pltpu.roll(keep_f, step, 0), 0.0)
        high = row < blocks - step
        end_b = end_b + jnp.where(high, keep_b * pltpu.roll(end_b, blocks - step, 0), 0.0)
        keep_b = jnp.where(high, keep_b * pltpu.roll(keep_b, blocks - step, 0), 0.0)
        step *= 2
    state_f = jnp.where(row >= 1, pltpu.roll(end_f, 1, 0), 0.0)
    state_b = jnp.where(row < blocks - 1, pltpu.roll(end_b, blocks - 1, 0), 0.0)
    sf = halves(state_f)
    sb = halves(state_b)
    if STAGE < 6:
        zs[0:LANES, :] = sf[0].astype(F32) + sf[1].astype(F32)
        zs[0:LANES, :] = sb[0].astype(F32) + sb[1].astype(F32)
        return

    zero = jnp.zeros((blocks, LANES), BF16)
    every = jnp.concatenate([sf[0], sf[1], sb[0], sb[1]], axis=1)
    pick_row = lax.broadcasted_iota(jnp.int32, (4 * LANES, LANES), 0)
    pick_col = lax.broadcasted_iota(jnp.int32, (4 * LANES, LANES), 1)
    target = STATE + (pick_row // LANES) * MODES + lax.rem(pick_row, LANES) // OWN
    lands = pick_col == target
    pick_mine = lax.rem(pick_row, OWN)
    for c in range(OWN):
        strip = jnp.broadcast_to(taps[c : c + 1, :], (LANES, LANES))
        strip = pltpu.roll(strip, 0, 1, stride=1, stride_axis=0)
        strip = jnp.where(col >= row, strip, 0.0)
        kern = halves(strip)
        nrek = halves(strip.T)
        of_c = mine == c
        uc = u[pl.ds(c, blocks, stride=OWN), :].astype(BF16)
        dc = dz[pl.ds(c, blocks, stride=OWN), :].astype(BF16)
        fh, fl = [jnp.where(of_c, x, zero) for x in sf]
        bh, bl = [jnp.where(of_c, x, zero) for x in sb]
        both = jnp.concatenate([uc, fh], axis=1)
        zc = dot(both, jnp.concatenate([kern[0], lead_f[0]], axis=0))
        zc = zc + dot(both, jnp.concatenate([kern[1], lead_f[1]], axis=0))
        zs[pl.ds(c, blocks, stride=OWN), :] = zc + dot(fl, lead_f[0])
        both = jnp.concatenate([dc, bh], axis=1)
        rc = dot(both, jnp.concatenate([nrek[0], lead_b[0]], axis=0))
        rc = rc + dot(both, jnp.concatenate([nrek[1], lead_b[1]], axis=0))
        ds[pl.ds(c, blocks, stride=OWN), :] = rc + dot(bl, lead_b[0])
        few = fixf[pl.ds(c, nseq, stride=OWN), :].astype(BF16)
        fixf[pl.ds(c, nseq, stride=OWN), :] = dot(few, kern[0]) + dot(few, kern[1])
        few = fixb[pl.ds(c, nseq, stride=OWN), :].astype(BF16)
        fixb[pl.ds(c, nseq, stride=OWN), :] = dot(few, nrek[0]) + dot(few, nrek[1])
        pick = jnp.where(lands & (pick_mine == c), 1.0, 0.0).astype(BF16)
        pay[pl.ds(c, blocks, stride=OWN), :] = dot(every, pick)
    if STAGE < 7:
        return
    for n in range(nseq):
        b = starts[n] // TOK
        rows = pl.ds(pl.multiple_of(b * SUB, SUB), SUB)
        place = b * TOK + lane
        fresh = (place >= starts[n]) & (place < starts[n + 1])
        zs[rows, :] = jnp.where(fresh, fixf[n * SUB : (n + 1) * SUB, :], zs[rows, :])
        if n > 0:
            fresh = (place >= starts[n - 1]) & (place < starts[n])
            ds[rows, :] = jnp.where(fresh, fixb[n * SUB : (n + 1) * SUB, :], ds[rows, :])
    if STAGE < 8:
        return

    def gradient_group(n, acc):
        acc = list(acc)
        for g in range(GROUP):
            b = n * GROUP + g
            rows = pl.ds(pl.multiple_of(b * SUB, SUB), SUB)
            now = moved[b].astype(F32)
            z = rounded(zs[rows, :])
            d = rounded(ds[rows, :])
            df = (now[24:32] * z, d * vc[rows, :], d * kc[rows, :])
            for i in range(3):
                f = i * TAPS
                acc[f] = acc[f] + df[i] * now[ROWS_OF[i] : ROWS_OF[i] + 8]
                for j in range(1, TAPS):
                    acc[f + j] = acc[f + j] + df[i] * sh[i * REACH + j - 1, b]
            halo = jnp.where(lane < REACH, df[0], 0.0)
            for i in (1, 2):
                part = pltpu.roll(df[i], i * REACH, 1)
                halo = jnp.where((lane >= i * REACH) & (lane < (i + 1) * REACH), part, halo)
            halos[rows, :] = halo
        return tuple(acc)

    acc = lax.fori_loop(
        0,
        blocks // GROUP,
        gradient_group,
        tuple(jnp.zeros((SUB, LANES), F32) for _ in range(3 * TAPS)),
    )
    grads = jnp.zeros((SUB, LANES), F32)
    for f in range(3 * TAPS):
        grads = jnp.where(lane == GRADS + f, jnp.sum(acc[f], axis=1, keepdims=True), grads)
    if STAGE < 9:
        zs[0:8, :] = grads
        return

    def finish_group(n, _):
        b0 = n * GROUP
        held = [moved[jnp.maximum(b0 - 1, 0)].astype(F32)]
        held += [moved[b0 + g].astype(F32) for g in range(GROUP - 1)]
        tiles = []
        for g in range(GROUP):
            b = b0 + g
            after = jnp.minimum(b + 1, blocks - 1)
            value = pay[pl.ds(pl.multiple_of(b * SUB, SUB), SUB), :] + grads
            value = value + halos[pl.ds(pl.multiple_of(after * SUB, SUB), SUB), :]
            for i in range(3):
                x = held[g][ROWS_OF[i] : ROWS_OF[i] + 8]
                first = LEFT + i * REACH
                x = x if i == 2 else pltpu.roll(x, first - (TOK - REACH) + LANES, 1)
                value = jnp.where((lane >= first) & (lane < first + REACH), x, value)
            tiles.append(value)
        for g in range(0, GROUP, 2):
            rows = pl.ds(pl.multiple_of((b0 + g) * SUB, 16), 16)
            out[rows, :] = jnp.concatenate(tiles[g : g + 2], axis=0).astype(BF16)
        return 0

    lax.fori_loop(0, blocks // GROUP, finish_group, 0)


def put(ref, t, value):
    ref[pl.ds(pl.multiple_of(t * SUB, SUB), SUB), :] = value


def at(ref, t):
    return ref[pl.ds(pl.multiple_of(t * SUB, SUB), SUB), :]


def put3(ref, i, t, value):
    ref[i, pl.ds(pl.multiple_of(t * SUB, SUB), SUB), :] = value


def at3(ref, i, t):
    return ref[i, pl.ds(pl.multiple_of(t * SUB, SUB), SUB), :]


def tile(ref, n):
    return ref[pl.ds(n * SUB, SUB), :]


def local_starts(total, seq):
    index = lax.axis_index("ctx")
    local = [s - index * TOK for s in start_list(seq)]
    local[-1] = total - index * TOK
    return local


def since(local, t):
    last = local[0]
    for s in local[1:]:
        last = jnp.where(s <= t, s, last)
    return t - last


def until(local, t):
    following = local[-1]
    for s in local[-2::-1]:
        following = jnp.where(s > t, s, following)
    return following - t


def near(local, t0):
    found = jnp.bool_(False)
    for s in local:
        found = found | ((s >= t0 - REACH) & (s < t0 + 8 + REACH + 1))
    return found


def eight_filtered(local, xs, ws, base, t0, masked):
    ages = [since(local, t0 + r) for r in range(8)] if masked else None
    done = []
    for i in range(3):
        w = [tile(ws, i * 8 + j) for j in range(TAPS)]
        x = [at3(xs, i, t0 + base - REACH + n) for n in range(8 + REACH)]
        row = []
        for r in range(8):
            acc = w[0] * x[r + REACH]
            for j in range(1, TAPS):
                term = w[j] * x[r + REACH - j]
                if masked:
                    term = jnp.where(ages[r] >= j, term, 0.0)
                acc = acc + term
            row.append(acc)
        done.append(row)
    return done


def prepare_kernel(
    total, seq, streams, cotangent, weight, rate, gain, qs, ks, vs, cots, heads, ws, prm, xs
):
    local = local_starts(total, seq)
    for k in range(SUB):
        cols = pl.ds(k * LANES, LANES)
        for g in range(MODES // 8):
            r = rate[g * 8 : g * 8 + 8, cols]
            prm[pl.ds(g * 64 + k, 8, stride=SUB), :] = jnp.exp(-r)
            prm[pl.ds(MODES * SUB + g * 64 + k, 8, stride=SUB), :] = gains(
                r, gain[g * 8 : g * 8 + 8, cols]
            )
        for i in range(3):
            ws[pl.ds(i * 64 + k, TAPS, stride=SUB), :] = weight[i, :, cols]
        for g in range(TOK // 16):
            some = pl.ds(g * 16, 16)
            for i in range(4):
                x = streams[i, some, cols] if i < 3 else cotangent[some, cols]
                x = x.astype(F32)
                for h in range(2):
                    rows = pl.ds((g * 16 + h * 8) * SUB + k, 8, stride=SUB)
                    part = x[h * 8 : h * 8 + 8]
                    if i == 3:
                        cots[rows, :] = part
                    else:
                        xs[i, rows, :] = part
                        if g == 0 and h == 0:
                            heads[i, rows, :] = part

    def filtering(t0, masked):
        done = eight_filtered(local, xs, ws, 0, t0, masked)
        for r in range(8):
            put(qs, t0 + r, done[0][r])
            put(ks, t0 + r, done[1][r])
            put(vs, t0 + r, done[2][r])

    def step(n, _):
        t0 = n * 8
        close = near(local, t0)

        @pl.when(close)
        def _():
            filtering(t0, True)

        @pl.when(jnp.logical_not(close))
        def _():
            filtering(t0, False)

        return 0

    lax.fori_loop(1, TOK // 8, step, 0)


def shard_kernel(
    total, seq, fields, qs, ks, vs, cots, heads, ws, prm, out, grads_out, wgrad,
    first, fs, q0, dzs, dfs, outs, sgs,
):
    local = local_starts(total, seq)
    for k in range(SUB):
        cols = pl.ds(k * LANES, LANES)
        turned = fields[pl.ds(k * LANES, LANES), :].astype(F32).T
        for g in range(LANES // 8):
            fs[pl.ds(g * 64 + k, 8, stride=SUB), :] = turned[g * 8 : g * 8 + 8]
    for i in range(3):
        first[i, 0 : REACH * SUB, :] = fs[(LEFT + i * REACH) * SUB : (LEFT + (i + 1) * REACH) * SUB, :]
        first[i, REACH * SUB : (REACH + 8) * SUB, :] = heads[i]
        dfs[i, TOK * SUB : (TOK + REACH) * SUB, :] = fs[
            (RIGHT + i * REACH) * SUB : (RIGHT + (i + 1) * REACH) * SUB, :
        ]
    done = eight_filtered(local, first, ws, REACH, 0, True)
    for i in range(3):
        for r in range(8):
            put3(q0, i, r, done[i][r])

    def forward(t0, state, masked, sources):
        q_ref, k_ref, v_ref = sources
        ages = [since(local, t0 + r) for r in range(8)] if masked else None
        state = list(state)
        for r in range(8):
            t = t0 + r
            q, c = at(q_ref, t), at(cots, t)
            put(dzs, t, rounded(c * q))
            u = rounded(at(k_ref, t) * at(v_ref, t))
            z = jnp.zeros((SUB, LANES), F32)
            for m in range(MODES):
                old = state[m]
                if masked:
                    old = jnp.where(ages[r] > 0, old, 0.0)
                state[m] = tile(prm, m) * old + u
                z = z + tile(prm, MODES + m) * state[m]
            z = rounded(z)
            put(outs, t, q * z)
            put3(dfs, 0, t, c * z)
        return tuple(state)

    def backward(t0, state, masked, sources):
        _, k_ref, v_ref = sources
        gaps = [until(local, t0 + r) for r in range(8)] if masked else None
        state = list(state)
        for r in range(7, -1, -1):
            t = t0 + r
            g = at(dzs, t)
            d = jnp.zeros((SUB, LANES), F32)
            for m in range(MODES):
                old = state[m]
                if masked:
                    old = jnp.where(gaps[r] > 1, old, 0.0)
                state[m] = tile(prm, m) * old + g
                d = d + tile(prm, MODES + m) * state[m]
            d = rounded(d)
            put3(dfs, 1, t, d * at(v_ref, t))
            put3(dfs, 2, t, d * at(k_ref, t))
        for i in range(3):
            w = [tile(ws, i * 8 + j) for j in range(TAPS)]
            y = [at3(dfs, i, t0 + n) for n in range(8 + REACH)]
            for r in range(8):
                acc = w[0] * y[r]
                for j in range(1, TAPS):
                    term = w[j] * y[r + j]
                    if masked:
                        term = jnp.where(gaps[r] > j, term, 0.0)
                    acc = acc + term
                put3(sgs, i, t0 + r, acc)
        return tuple(state)

    def entering(g):
        return tuple(
            tile(fs, STATE + g * MODES + m) + tile(fs, STATE + (g + 1) * MODES + m)
            for m in range(MODES)
        )

    edge = (q0.at[0], q0.at[1], q0.at[2])
    whole = (qs, ks, vs)

    def step_f(n, state):
        t0 = n * 8
        return lax.cond(
            near(local, t0),
            lambda s: forward(t0, s, True, whole),
            lambda s: forward(t0, s, False, whole),
            state,
        )

    def step_b(n, state):
        t0 = TOK - 8 - n * 8
        return lax.cond(
            near(local, t0),
            lambda s: backward(t0, s, True, whole),
            lambda s: backward(t0, s, False, whole),
            state,
        )

    state = forward(0, entering(0), True, edge)
    lax.fori_loop(1, TOK // 8, step_f, state)
    state = lax.fori_loop(0, TOK // 8 - 1, step_b, entering(2))
    backward(0, state, True, edge)

    for k in range(SUB):
        cols = pl.ds(k * LANES, LANES)
        for i in range(3):
            wgrad[i, :, cols] = fs[pl.ds((GRADS + i * TAPS) * SUB + k, TAPS, stride=SUB), :]
        for g in range(TOK // 16):
            for i in range(4):
                parts = []
                for h in range(2):
                    rows = pl.ds((g * 16 + h * 8) * SUB + k, 8, stride=SUB)
                    parts.append(sgs[i, rows, :] if i < 3 else outs[rows, :])
                both = jnp.concatenate(parts, axis=0).astype(BF16)
                if i < 3:
                    grads_out[i, pl.ds(g * 16, 16), cols] = both
                else:
                    out[pl.ds(g * 16, 16), cols] = both


def norm_kernel(fields, out):
    lane = lax.broadcasted_iota(jnp.int32, fields.shape, 1)
    value = fields[...].astype(F32)
    value = jnp.where((lane >= GRADS) & (lane < GRADS + 3 * TAPS), value, 0.0)
    out[...] = jnp.broadcast_to(jnp.sum(value * value), out.shape)


def clip_kernel(grads, squares, out):
    total = squares[0]
    for n in range(1, squares.shape[0]):
        total = total + squares[n]
    factor = jnp.minimum(F32(1.0), 1.0 / jnp.sqrt(total[0:1, :] + 1e-06))
    for k in range(grads.shape[2] // LANES):
        cols = pl.ds(k * LANES, LANES)
        for i in range(grads.shape[0]):
            out[i, :, cols] = grads[i, :, cols] * factor


def vmem():
    return pl.BlockSpec(memory_space=pltpu.VMEM)


def smem():
    return pl.BlockSpec(memory_space=pltpu.SMEM)


def body(streams, seq_lengths, conv_weight, rate, modal_gain, cotangent):
    tok, chans = streams.shape[1:]
    shards = lax.axis_size("ctx")
    total = tok * shards
    rate_t, gain_t = rate.T, modal_gain.T
    params = pltpu.CompilerParams(vmem_limit_bytes=48 * 1024 * 1024)
    turned = pl.pallas_call(
        turn_kernel,
        out_shape=jax.ShapeDtypeStruct((shards, 4 * OWN, tok), BF16),
        in_specs=[vmem()] * 2,
        out_specs=vmem(),
        compiler_params=params,
        name="turn",
    )(streams, cotangent)
    moved = lax.all_to_all(turned, "ctx", split_axis=0, concat_axis=0, tiled=True)
    plane = jax.ShapeDtypeStruct((tok * SUB, LANES), F32)
    prepared = pl.pallas_call(
        functools.partial(prepare_kernel, total),
        out_shape=[plane] * 4
        + [
            jax.ShapeDtypeStruct((3, 8 * SUB, LANES), F32),
            jax.ShapeDtypeStruct((3 * 8 * SUB, LANES), F32),
            jax.ShapeDtypeStruct((2 * MODES * SUB, LANES), F32),
        ],
        in_specs=[smem()] + [vmem()] * 5,
        out_specs=[vmem()] * 7,
        scratch_shapes=[pltpu.VMEM((3, tok * SUB, LANES), F32)],
        compiler_params=params,
        cost_estimate=pl.CostEstimate(flops=20_000_000, bytes_accessed=4_000_000, transcendentals=0),
        name="prepare",
    )(seq_lengths, streams, cotangent, conv_weight, rate_t, gain_t)
    moved, *prepared = lax.optimization_barrier((moved, *prepared))
    rows = shards * OWN
    plane = pltpu.VMEM((rows, LANES), F32)
    payload = pl.pallas_call(
        functools.partial(owner_kernel, total),
        out_shape=jax.ShapeDtypeStruct((rows, LANES), BF16),
        in_specs=[smem()] + [vmem()] * 4,
        out_specs=vmem(),
        scratch_shapes=[
            pltpu.VMEM((3 * REACH, shards, SUB, LANES), F32),
            pltpu.VMEM((3 * TAPS, SUB, LANES), F32),
        ]
        + [plane] * 8
        + [pltpu.VMEM((8 * SUB, LANES), F32)] * 2
        + [pltpu.VMEM((LANES, LANES), F32)],
        compiler_params=params,
        name="owner",
    )(seq_lengths, moved, conv_weight, rate_t, gain_t)
    fields = lax.all_to_all(
        payload.reshape(shards, OWN, LANES), "ctx", split_axis=0, concat_axis=0, tiled=True
    ).reshape(rows, LANES)
    planes = lax.axis_size("ch")
    partial = pl.pallas_call(
        norm_kernel,
        out_shape=jax.ShapeDtypeStruct((planes, SUB, LANES), F32),
        in_specs=[vmem()],
        out_specs=vmem(),
        name="norm",
    )(fields)
    squares = lax.all_to_all(partial, "ch", split_axis=0, concat_axis=0, tiled=True)
    scratch = pltpu.VMEM((tok * SUB, LANES), F32)
    output, stream_grads, weight_grad = pl.pallas_call(
        functools.partial(shard_kernel, total),
        out_shape=[
            jax.ShapeDtypeStruct((tok, chans), BF16),
            jax.ShapeDtypeStruct((3, tok, chans), BF16),
            jax.ShapeDtypeStruct((3, TAPS, chans), F32),
        ],
        in_specs=[smem()] + [vmem()] * 8,
        out_specs=[vmem()] * 3,
        scratch_shapes=[
            pltpu.VMEM((3, (REACH + 8) * SUB, LANES), F32),
            pltpu.VMEM((LANES * SUB, LANES), F32),
            pltpu.VMEM((3, 8 * SUB, LANES), F32),
            scratch,
            pltpu.VMEM((3, (tok + REACH) * SUB, LANES), F32),
            scratch,
            pltpu.VMEM((3, tok * SUB, LANES), F32),
        ],
        compiler_params=params,
        cost_estimate=pl.CostEstimate(flops=40_000_000, bytes_accessed=6_000_000, transcendentals=0),
        name="shard",
    )(seq_lengths, fields, *prepared)
    clipped = pl.pallas_call(
        clip_kernel,
        out_shape=jax.ShapeDtypeStruct(weight_grad.shape, F32),
        in_specs=[vmem()] * 2,
        out_specs=vmem(),
        name="clip",
    )(weight_grad, squares)
    return output, stream_grads, clipped


def solution(mesh):
    return jax.shard_map(
        body,
        mesh=mesh,
        in_specs=(
            P(None, "ctx", "ch"),
            P(),
            P(None, None, "ch"),
            P("ch", None),
            P("ch", None),
            P("ctx", "ch"),
        ),
        out_specs=(P("ctx", "ch"), P(None, "ctx", "ch"), P(None, None, "ch")),
        check_vma=False,
    )
```

```python
import functools

import jax
import jax.numpy as jnp
from jax import lax
from jax.experimental import pallas as pl
from jax.experimental.pallas import tpu as pltpu
from jax.sharding import PartitionSpec as P

F32 = jnp.float32
BF16 = jnp.bfloat16
TAPS = 7
REACH = TAPS - 1
TOK = 128
LANES = 128
OWN = 8
SUB = 8
GROUP = 64
TURNS = 4
PREPARED = 10
EDGE = 8
SPAN = 24

LEFT = LANES - 3 * REACH
RIGHT = 0
STATE = 18
MODES = 16
GRADS = STATE + 4 * MODES


def rounded(value):
    return value.astype(BF16).astype(F32)


def halves(value):
    high = value.astype(BF16)
    return high, (value - high.astype(F32)).astype(BF16)


def one_minus_exp(x):
    series = jnp.full_like(x, 1.0)
    for n in range(11, 1, -1):
        series = 1.0 - (x * F32(1.0 / n)) * series
    return x * series


def gains(rate, gain):
    return gain * jnp.sqrt(one_minus_exp(2.0 * rate))


def start_list(seq_ref):
    starts = [jnp.int32(0)]
    for n in range(seq_ref.shape[0]):
        starts.append(starts[-1] + seq_ref[n])
    return starts


def dot(a, b):
    return lax.dot_general(a, b, (((1,), (0,)), ((), ())), preferred_element_type=F32)


def dot_t(a, b):
    return lax.dot_general(a, b, (((1,), (1,)), ((), ())), preferred_element_type=F32)


def turn_kernel(streams, cotangent, out, held, turned, arrive, leave):
    wide = held.shape[3]
    owners = wide // OWN
    coming = []
    for n in range(TURNS):
        cols = pl.ds(n * wide, wide)
        coming.append(
            (
                pltpu.make_async_copy(streams.at[:, :, cols], held.at[n, 0:3], arrive.at[n, 0]),
                pltpu.make_async_copy(cotangent.at[:, cols], held.at[n, 3], arrive.at[n, 1]),
            )
        )
        for copy in coming[-1]:
            copy.start()
    going = []
    for n in range(TURNS):
        for copy in coming[n]:
            copy.wait()
        for pair in range(2):
            for k in range(wide // LANES):
                cols = pl.ds(k * LANES, LANES)
                a, b = [
                    held[n, 2 * pair + i, :, cols].astype(F32).T.reshape(LANES // OWN, OWN, TOK)
                    for i in (0, 1)
                ]
                rows = pl.ds(n * owners + k * (LANES // OWN), LANES // OWN)
                turned[rows, pl.ds(pair * 16, 16), :] = jnp.concatenate([a, b], axis=1).astype(BF16)
        some = pl.ds(n * owners, owners)
        going.append(pltpu.make_async_copy(turned.at[some], out.at[some], leave.at[n]))
        going[-1].start()
    for copy in going:
        copy.wait()


ROWS_OF = (0, 8, 16, 24)


def owner_kernel(
    total, seq, moved, weight, rate, gain, out, sh, wide, u, dz, kc, vc, zs, ds, pay, halos, fixf, fixb, prm
):
    blocks = moved.shape[0]
    index = lax.axis_index("ctx")
    starts = start_list(seq)
    starts[-1] = jnp.int32(total)
    nseq = seq.shape[0]
    lane = lax.broadcasted_iota(jnp.int32, (SUB, LANES), 1)

    chunk = pl.multiple_of((index // (LANES // OWN)) * LANES, LANES)
    back = lax.rem(LANES - lax.rem(index, LANES // OWN) * OWN, LANES)
    cols = pl.ds(chunk, LANES)
    prm[...] = jnp.zeros_like(prm)
    prm[0:MODES, :] = pltpu.roll(rate[:, cols], back, 1)
    prm[MODES : 2 * MODES, :] = pltpu.roll(gain[:, cols], back, 1)
    for i in range(3):
        prm[32 + 8 * i : 32 + 8 * i + TAPS, :] = weight[i, :, cols]
    prm[32:56, :] = pltpu.roll(prm[32:56, :], back, 1)
    own = prm[...].T[0:OWN, :]
    for i in range(3):
        for j in range(TAPS):
            f = 32 + 8 * i + j
            wide[i * TAPS + j] = jnp.broadcast_to(own[:, f : f + 1], (SUB, LANES))
    rate_rows = jnp.concatenate(
        [jnp.broadcast_to(own[:, m : m + 1], (SUB, LANES)) for m in range(MODES)], axis=0
    )
    gain_rows = jnp.concatenate(
        [
            jnp.broadcast_to(own[:, MODES + m : MODES + m + 1], (SUB, LANES))
            for m in range(MODES)
        ],
        axis=0,
    )
    coef_rows = gains(rate_rows, gain_rows)

    def filtering(b, now, before, since):
        done = []
        for i in range(3):
            x = now[ROWS_OF[i] : ROWS_OF[i] + 8]
            p = before[ROWS_OF[i] : ROWS_OF[i] + 8]
            acc = wide[i * TAPS] * x
            for j in range(1, TAPS):
                moved_x = pltpu.roll(jnp.where(lane >= LANES - j, p, x), j, 1)
                if since is not None:
                    moved_x = jnp.where(since >= j, moved_x, 0.0)
                sh[i * REACH + j - 1, b] = moved_x
                acc = acc + wide[i * TAPS + j] * moved_x
            done.append(acc)
        rows = pl.ds(pl.multiple_of(b * SUB, SUB), SUB)
        u[rows, :] = rounded(done[1] * done[2])
        dz[rows, :] = rounded(now[24:32] * done[0])
        kc[rows, :] = done[1]
        vc[rows, :] = done[2]

    def filter_group(n, _):
        b0 = n * GROUP
        held = [moved[jnp.maximum(b0 - 1, 0)].astype(F32)]
        held += [moved[b0 + g].astype(F32) for g in range(GROUP)]
        for g in range(GROUP):
            filtering(b0 + g, held[g + 1], held[g], None)
        return 0

    lax.fori_loop(0, blocks // GROUP, filter_group, 0)
    for s in starts[:-1]:
        for near in (0, 1):
            b = jnp.minimum(s // TOK + near, blocks - 1)
            place = b * TOK + lane
            since = jnp.zeros((SUB, LANES), jnp.int32)
            for other in starts[:-1]:
                since = jnp.where(other <= place, other, since)
            filtering(
                b,
                moved[b].astype(F32),
                moved[jnp.maximum(b - 1, 0)].astype(F32),
                place - since,
            )

    for n in range(nseq):
        b = starts[n] // TOK
        rows = pl.ds(pl.multiple_of(b * SUB, SUB), SUB)
        place = b * TOK + lane
        fixf[n * SUB : (n + 1) * SUB, :] = jnp.where(place >= starts[n], u[rows, :], 0.0)
        fixb[n * SUB : (n + 1) * SUB, :] = jnp.where(place < starts[n], dz[rows, :], 0.0)

    row = lax.broadcasted_iota(jnp.int32, (blocks, TOK), 0)
    col = lax.broadcasted_iota(jnp.int32, (blocks, TOK), 1)
    head = jnp.ones((blocks, TOK), F32)
    tail = jnp.ones((blocks, TOK), F32)
    spot = row * TOK + col
    for s in starts[:-1]:
        base = s - lax.rem(s, TOK)
        head = jnp.where((spot >= s) & (spot < base + TOK), 0.0, head)
        tail = jnp.where((spot < s) & (spot >= base), 0.0, tail)

    lag = col.astype(F32)
    ending = halves(jnp.exp(-rate_rows * (TOK - 1.0 - lag)))
    falling = jnp.exp(-rate_rows * lag)
    opening = halves(falling)
    lead_f = halves(coef_rows * jnp.exp(-rate_rows * (lag + 1.0)))
    lead_b = halves(coef_rows * jnp.exp(-rate_rows * (TOK - lag)))
    whole = jnp.exp(-rate_rows * TOK).T[0:1, :]
    taps = (coef_rows * falling).reshape(MODES, OWN, LANES).sum(axis=0)

    mine = lax.rem(col, OWN)
    ending = jnp.concatenate(ending, axis=1)
    opening = jnp.concatenate(opening, axis=1)
    end_f = jnp.zeros((blocks, LANES), F32)
    end_b = jnp.zeros((blocks, LANES), F32)
    for c in range(OWN):
        uc = (u[pl.ds(c, blocks, stride=OWN), :] * tail).astype(BF16)
        dc = (dz[pl.ds(c, blocks, stride=OWN), :] * head).astype(BF16)
        ef = dot_t(jnp.concatenate([uc, uc], axis=1), ending)
        eb = dot_t(jnp.concatenate([dc, dc], axis=1), opening)
        end_f = jnp.where(mine == c, ef, end_f)
        end_b = jnp.where(mine == c, eb, end_b)

    keep_f = head[:, TOK - 1 : TOK] * whole
    keep_b = keep_f
    step = 1
    while step < blocks:
        low = row >= step
        end_f = end_f + jnp.where(low, keep_f * pltpu.roll(end_f, step, 0), 0.0)
        keep_f = jnp.where(low, keep_f * pltpu.roll(keep_f, step, 0), 0.0)
        high = row < blocks - step
        end_b = end_b + jnp.where(high, keep_b * pltpu.roll(end_b, blocks - step, 0), 0.0)
        keep_b = jnp.where(high, keep_b * pltpu.roll(keep_b, blocks - step, 0), 0.0)
        step *= 2
    state_f = jnp.where(row >= 1, pltpu.roll(end_f, 1, 0), 0.0)
    state_b = jnp.where(row < blocks - 1, pltpu.roll(end_b, blocks - 1, 0), 0.0)
    sf = halves(state_f)
    sb = halves(state_b)

    zero = jnp.zeros((blocks, LANES), BF16)
    every = jnp.concatenate([sf[0], sf[1], sb[0], sb[1]], axis=1)
    pick_row = lax.broadcasted_iota(jnp.int32, (4 * LANES, LANES), 0)
    pick_col = lax.broadcasted_iota(jnp.int32, (4 * LANES, LANES), 1)
    target = STATE + (pick_row // LANES) * MODES + lax.rem(pick_row, LANES) // OWN
    lands = pick_col == target
    pick_mine = lax.rem(pick_row, OWN)
    for c in range(OWN):
        strip = jnp.broadcast_to(taps[c : c + 1, :], (LANES, LANES))
        strip = pltpu.roll(strip, 0, 1, stride=1, stride_axis=0)
        strip = jnp.where(col >= row, strip, 0.0)
        kern = halves(strip)
        nrek = halves(strip.T)
        of_c = mine == c
        uc = u[pl.ds(c, blocks, stride=OWN), :].astype(BF16)
        dc = dz[pl.ds(c, blocks, stride=OWN), :].astype(BF16)
        fh, fl = [jnp.where(of_c, x, zero) for x in sf]
        bh, bl = [jnp.where(of_c, x, zero) for x in sb]
        both = jnp.concatenate([uc, fh], axis=1)
        zc = dot(both, jnp.concatenate([kern[0], lead_f[0]], axis=0))
        zc = zc + dot(both, jnp.concatenate([kern[1], lead_f[1]], axis=0))
        zs[pl.ds(c, blocks, stride=OWN), :] = zc + dot(fl, lead_f[0])
        both = jnp.concatenate([dc, bh], axis=1)
        rc = dot(both, jnp.concatenate([nrek[0], lead_b[0]], axis=0))
        rc = rc + dot(both, jnp.concatenate([nrek[1], lead_b[1]], axis=0))
        ds[pl.ds(c, blocks, stride=OWN), :] = rc + dot(bl, lead_b[0])
        few = fixf[pl.ds(c, nseq, stride=OWN), :].astype(BF16)
        fixf[pl.ds(c, nseq, stride=OWN), :] = dot(few, kern[0]) + dot(few, kern[1])
        few = fixb[pl.ds(c, nseq, stride=OWN), :].astype(BF16)
        fixb[pl.ds(c, nseq, stride=OWN), :] = dot(few, nrek[0]) + dot(few, nrek[1])
        pick = jnp.where(lands & (pick_mine == c), 1.0, 0.0).astype(BF16)
        pay[pl.ds(c, blocks, stride=OWN), :] = dot(every, pick)
    for n in range(nseq):
        b = starts[n] // TOK
        rows = pl.ds(pl.multiple_of(b * SUB, SUB), SUB)
        place = b * TOK + lane
        fresh = (place >= starts[n]) & (place < starts[n + 1])
        zs[rows, :] = jnp.where(fresh, fixf[n * SUB : (n + 1) * SUB, :], zs[rows, :])
        if n > 0:
            fresh = (place >= starts[n - 1]) & (place < starts[n])
            ds[rows, :] = jnp.where(fresh, fixb[n * SUB : (n + 1) * SUB, :], ds[rows, :])

    def gradient_group(n, acc):
        acc = list(acc)
        for g in range(GROUP):
            b = n * GROUP + g
            rows = pl.ds(pl.multiple_of(b * SUB, SUB), SUB)
            now = moved[b].astype(F32)
            z = rounded(zs[rows, :])
            d = rounded(ds[rows, :])
            df = (now[24:32] * z, d * vc[rows, :], d * kc[rows, :])
            for i in range(3):
                f = i * TAPS
                acc[f] = acc[f] + df[i] * now[ROWS_OF[i] : ROWS_OF[i] + 8]
                for j in range(1, TAPS):
                    acc[f + j] = acc[f + j] + df[i] * sh[i * REACH + j - 1, b]
            halo = jnp.where(lane < REACH, df[0], 0.0)
            for i in (1, 2):
                part = pltpu.roll(df[i], i * REACH, 1)
                halo = jnp.where((lane >= i * REACH) & (lane < (i + 1) * REACH), part, halo)
            halos[rows, :] = halo
        return tuple(acc)

    acc = lax.fori_loop(
        0,
        blocks // GROUP,
        gradient_group,
        tuple(jnp.zeros((SUB, LANES), F32) for _ in range(3 * TAPS)),
    )
    grads = jnp.zeros((SUB, LANES), F32)
    for f in range(3 * TAPS):
        grads = jnp.where(lane == GRADS + f, jnp.sum(acc[f], axis=1, keepdims=True), grads)

    def finish_group(n, _):
        b0 = n * GROUP
        held = [moved[jnp.maximum(b0 - 1, 0)].astype(F32)]
        held += [moved[b0 + g].astype(F32) for g in range(GROUP - 1)]
        tiles = []
        for g in range(GROUP):
            b = b0 + g
            after = jnp.minimum(b + 1, blocks - 1)
            value = pay[pl.ds(pl.multiple_of(b * SUB, SUB), SUB), :] + grads
            value = value + halos[pl.ds(pl.multiple_of(after * SUB, SUB), SUB), :]
            for i in range(3):
                x = held[g][ROWS_OF[i] : ROWS_OF[i] + 8]
                first = LEFT + i * REACH
                x = x if i == 2 else pltpu.roll(x, first - (TOK - REACH) + LANES, 1)
                value = jnp.where((lane >= first) & (lane < first + REACH), x, value)
            tiles.append(value)
        for g in range(0, GROUP, 2):
            rows = pl.ds(pl.multiple_of((b0 + g) * SUB, 16), 16)
            out[rows, :] = jnp.concatenate(tiles[g : g + 2], axis=0).astype(BF16)
        return 0

    lax.fori_loop(0, blocks // GROUP, finish_group, 0)


def put(ref, t, value):
    ref[pl.ds(pl.multiple_of(t * SUB, SUB), SUB), :] = value


def at(ref, t):
    return ref[pl.ds(pl.multiple_of(t * SUB, SUB), SUB), :]


def put3(ref, i, t, value):
    ref[i, pl.ds(pl.multiple_of(t * SUB, SUB), SUB), :] = value


def at3(ref, i, t):
    return ref[i, pl.ds(pl.multiple_of(t * SUB, SUB), SUB), :]


def tile(ref, n):
    return ref[pl.ds(n * SUB, SUB), :]


def local_starts(total, seq):
    index = lax.axis_index("ctx")
    local = [s - index * TOK for s in start_list(seq)]
    local[-1] = total - index * TOK
    return local


def since(local, t):
    last = local[0]
    for s in local[1:]:
        last = jnp.where(s <= t, s, last)
    return t - last


def until(local, t):
    following = local[-1]
    for s in local[-2::-1]:
        following = jnp.where(s > t, s, following)
    return following - t


def near(local, t0, count):
    found = jnp.bool_(False)
    for s in local:
        found = found | ((s >= t0 - REACH) & (s < t0 + count + REACH + 1))
    return found


def added(terms):
    while len(terms) > 1:
        rest = terms[len(terms) // 2 * 2 :]
        terms = [a + b for a, b in zip(terms[0::2], terms[1::2])] + rest
    return terms[0]


def scanned(prm, state, value, alive):
    for m in range(MODES):
        old = state[m]
        if alive is not None:
            old = jnp.where(alive, old, 0.0)
        state[m] = tile(prm, m) * old + value
    return added([tile(prm, MODES + m) * state[m] for m in range(MODES)])


def carried(prm, state, alive):
    for m in range(MODES):
        old = state[m]
        if alive is not None:
            old = jnp.where(alive, old, 0.0)
        state[m] = tile(prm, m) * old
    return added(list(state))


def eight_filtered(local, xs, ws, base, t0, masked):
    ages = [since(local, t0 + r) for r in range(8)] if masked else None
    done = []
    for i in range(3):
        w = [tile(ws, i * 8 + j) for j in range(TAPS)]
        x = [at3(xs, i, t0 + base - REACH + n) for n in range(8 + REACH)]
        row = []
        for r in range(8):
            acc = w[0] * x[r + REACH]
            for j in range(1, TAPS):
                term = w[j] * x[r + REACH - j]
                if masked:
                    term = jnp.where(ages[r] >= j, term, 0.0)
                acc = acc + term
            row.append(acc)
        done.append(row)
    return done


def prepare_kernel(
    total, seq, streams, cotangent, weight, rate, gain,
    heads, ws, prm, qs, zl, cots, ks, vs, dl, rl, xs, dzs,
):
    local = local_starts(total, seq)
    for k in range(SUB):
        cols = pl.ds(k * LANES, LANES)
        for g in range(MODES // 8):
            r = rate[g * 8 : g * 8 + 8, cols]
            prm[pl.ds(g * 64 + k, 8, stride=SUB), :] = jnp.exp(-r)
            prm[pl.ds(MODES * SUB + g * 64 + k, 8, stride=SUB), :] = gains(
                r, gain[g * 8 : g * 8 + 8, cols]
            )
        for i in range(3):
            ws[pl.ds(i * 64 + k, TAPS, stride=SUB), :] = weight[i, :, cols]
        for g in range(TOK // 16):
            some = pl.ds(g * 16, 16)
            for i in range(4):
                x = streams[i, some, cols] if i < 3 else cotangent[some, cols]
                x = x.astype(F32)
                for h in range(2):
                    rows = pl.ds((g * 16 + h * 8) * SUB + k, 8, stride=SUB)
                    part = x[h * 8 : h * 8 + 8]
                    if i == 3:
                        cots[rows, :] = part
                    else:
                        xs[i, rows, :] = part
                        if g == 0 and h == 0:
                            heads[i, rows, :] = part
    for ref in (qs, ks, vs, zl, dl):
        ref[0 : EDGE * SUB, :] = jnp.zeros((EDGE * SUB, LANES), F32)

    def forward(t0, state, masked):
        done = eight_filtered(local, xs, ws, 0, t0, masked)
        state = list(state)
        for r in range(8):
            t = t0 + r
            q, k, v = done[0][r], done[1][r], done[2][r]
            put(qs, t, q)
            put(ks, t, k)
            put(vs, t, v)
            put(dzs, t, rounded(at(cots, t) * q))
            alive = since(local, t) > 0 if masked else None
            put(zl, t, scanned(prm, state, rounded(k * v), alive))
        return tuple(state)

    def backward(t0, state, masked):
        state = list(state)
        for r in range(7, -1, -1):
            t = t0 + r
            alive = until(local, t) > 1 if masked else None
            put(dl, t, scanned(prm, state, at(dzs, t), alive))
        return tuple(state)

    def either(kernel, t0, state):
        return lax.cond(
            near(local, t0, 8),
            lambda s: kernel(t0, s, True),
            lambda s: kernel(t0, s, False),
            state,
        )

    zeros = tuple(jnp.zeros((SUB, LANES), F32) for _ in range(MODES))
    steps = (TOK - EDGE) // 8
    lax.fori_loop(0, steps, lambda n, s: either(forward, EDGE + n * 8, s), zeros)
    state = lax.fori_loop(0, steps, lambda n, s: either(backward, TOK - 8 - n * 8, s), zeros)
    for m in range(MODES):
        put(rl, m, state[m])


def shard_kernel(total, seq, *refs):
    far, refs = refs[: 1 + PREPARED], refs[1 + PREPARED :]
    out, grads_out, wgrad, *refs = refs
    held, refs = refs[: 1 + PREPARED], refs[1 + PREPARED :]
    arrive, first, fs, q0, dz0, dfs, outs, sgs = refs
    fields, heads, ws, prm, qs, zl, cots, ks, vs, dl, rl = held
    coming = []
    for n in range(1 + PREPARED):
        coming.append(pltpu.make_async_copy(far[n], held[n], arrive.at[n]))
        coming[-1].start()
    local = local_starts(total, seq)
    coming[0].wait()
    for k in range(SUB):
        cols = pl.ds(k * LANES, LANES)
        turned = fields[pl.ds(k * LANES, LANES), :].astype(F32).T
        for g in range(LANES // 8):
            fs[pl.ds(g * 64 + k, 8, stride=SUB), :] = turned[g * 8 : g * 8 + 8]
    for copy in coming[1:7]:
        copy.wait()
    for i in range(3):
        first[i, 0 : REACH * SUB, :] = fs[(LEFT + i * REACH) * SUB : (LEFT + (i + 1) * REACH) * SUB, :]
        first[i, REACH * SUB : (REACH + EDGE) * SUB, :] = heads[i]
        dfs[i, TOK * SUB : (TOK + REACH) * SUB, :] = fs[
            (RIGHT + i * REACH) * SUB : (RIGHT + (i + 1) * REACH) * SUB, :
        ]

    def entering(g):
        return [
            tile(fs, STATE + g * MODES + m) + tile(fs, STATE + (g + 1) * MODES + m)
            for m in range(MODES)
        ]

    def settle(t, q, z):
        z = rounded(z)
        put(outs, t, q * z)
        put3(dfs, 0, t, at(cots, t) * z)

    def settle_back(t, k, v, d):
        d = rounded(d)
        put3(dfs, 1, t, d * v)
        put3(dfs, 2, t, d * k)

    def adjoint(t0, count, masked):
        gaps = [until(local, t0 + r) for r in range(count)] if masked else None
        for i in range(3):
            w = [tile(ws, i * 8 + j) for j in range(TAPS)]
            y = [at3(dfs, i, t0 + n) for n in range(count + REACH)]
            for r in range(count):
                acc = w[0] * y[r]
                for j in range(1, TAPS):
                    term = w[j] * y[r + j]
                    if masked:
                        term = jnp.where(gaps[r] > j, term, 0.0)
                    acc = acc + term
                put3(sgs, i, t0 + r, acc)

    def forward(t0, state, masked):
        state = list(state)
        for r in range(SPAN):
            t = t0 + r
            alive = since(local, t) > 0 if masked else None
            settle(t, at(qs, t), at(zl, t) + carried(prm, state, alive))
        return tuple(state)

    def backward(t0, state, masked):
        state = list(state)
        for r in range(SPAN - 1, -1, -1):
            t = t0 + r
            alive = until(local, t) > 1 if masked else None
            settle_back(t, at(ks, t), at(vs, t), at(dl, t) + carried(prm, state, alive))
        adjoint(t0, SPAN, masked)
        return tuple(state)

    def either(kernel, t0, state):
        return lax.cond(
            near(local, t0, SPAN),
            lambda s: kernel(t0, s, True),
            lambda s: kernel(t0, s, False),
            state,
        )

    def weighted(state):
        return tuple(tile(prm, MODES + m) * state[m] for m in range(MODES))

    done = eight_filtered(local, first, ws, REACH, 0, True)
    state = entering(0)
    for t in range(EDGE):
        q, k, v = done[0][t], done[1][t], done[2][t]
        put(dz0, t, rounded(at(cots, t) * q))
        put3(q0, 0, t, k)
        put3(q0, 1, t, v)
        settle(t, q, scanned(prm, state, rounded(k * v), since(local, t) > 0))
    steps = (TOK - EDGE) // SPAN
    lax.fori_loop(0, steps, lambda n, s: either(forward, EDGE + n * SPAN, s), weighted(state))
    for copy in coming[7:]:
        copy.wait()
    carry = lax.fori_loop(
        0,
        steps,
        lambda n, s: either(backward, TOK - (n + 1) * SPAN, s),
        weighted(entering(2)),
    )
    carry = list(carry)
    state = [tile(rl, m) for m in range(MODES)]
    for t in range(EDGE - 1, -1, -1):
        alive = until(local, t) > 1
        d = scanned(prm, state, at(dz0, t), alive) + carried(prm, carry, alive)
        settle_back(t, at3(q0, 0, t), at3(q0, 1, t), d)
    adjoint(0, EDGE, True)

    for k in range(SUB):
        cols = pl.ds(k * LANES, LANES)
        for i in range(3):
            wgrad[i, :, cols] = fs[pl.ds((GRADS + i * TAPS) * SUB + k, TAPS, stride=SUB), :]
        for g in range(TOK // 16):
            for i in range(4):
                parts = []
                for h in range(2):
                    rows = pl.ds((g * 16 + h * 8) * SUB + k, 8, stride=SUB)
                    parts.append(sgs[i, rows, :] if i < 3 else outs[rows, :])
                both = jnp.concatenate(parts, axis=0).astype(BF16)
                if i < 3:
                    grads_out[i, pl.ds(g * 16, 16), cols] = both
                else:
                    out[pl.ds(g * 16, 16), cols] = both


def norm_kernel(fields, out):
    lane = lax.broadcasted_iota(jnp.int32, fields.shape, 1)
    value = fields[...].astype(F32)
    value = jnp.where((lane >= GRADS) & (lane < GRADS + 3 * TAPS), value, 0.0)
    out[...] = jnp.broadcast_to(jnp.sum(value * value), out.shape)


def clip_kernel(grads, squares, out):
    total = squares[0]
    for n in range(1, squares.shape[0]):
        total = total + squares[n]
    factor = jnp.minimum(F32(1.0), 1.0 / jnp.sqrt(total[0:1, :] + 1e-06))
    for k in range(grads.shape[2] // LANES):
        cols = pl.ds(k * LANES, LANES)
        for i in range(grads.shape[0]):
            out[i, :, cols] = grads[i, :, cols] * factor


def params(mebibytes):
    return pltpu.CompilerParams(vmem_limit_bytes=mebibytes * 1024 * 1024)


def vmem():
    return pl.BlockSpec(memory_space=pltpu.VMEM)


def smem():
    return pl.BlockSpec(memory_space=pltpu.SMEM)


def body(streams, seq_lengths, conv_weight, rate, modal_gain, cotangent):
    tok, chans = streams.shape[1:]
    shards = lax.axis_size("ctx")
    total = tok * shards
    rate_t, gain_t = rate.T, modal_gain.T
    turned = pl.pallas_call(
        turn_kernel,
        out_shape=jax.ShapeDtypeStruct((shards, 4 * OWN, tok), BF16),
        in_specs=[pl.BlockSpec(memory_space=pl.ANY)] * 2,
        out_specs=pl.BlockSpec(memory_space=pl.ANY),
        scratch_shapes=[
            pltpu.VMEM((TURNS, 4, tok, chans // TURNS), BF16),
            pltpu.VMEM((shards, 4 * OWN, tok), BF16),
            pltpu.SemaphoreType.DMA((TURNS, 2)),
            pltpu.SemaphoreType.DMA((TURNS,)),
        ],
        compiler_params=params(60),
        name="turn",
    )(streams, cotangent)
    moved = lax.all_to_all(turned, "ctx", split_axis=0, concat_axis=0, tiled=True)
    plane = jax.ShapeDtypeStruct((tok * SUB, LANES), F32)
    scratch = pltpu.VMEM((tok * SUB, LANES), F32)
    prepared = pl.pallas_call(
        functools.partial(prepare_kernel, total),
        out_shape=[
            jax.ShapeDtypeStruct((3, EDGE * SUB, LANES), F32),
            jax.ShapeDtypeStruct((3 * 8 * SUB, LANES), F32),
            jax.ShapeDtypeStruct((2 * MODES * SUB, LANES), F32),
        ]
        + [plane] * 6
        + [jax.ShapeDtypeStruct((MODES * SUB, LANES), F32)],
        in_specs=[smem()] + [vmem()] * 5,
        out_specs=[vmem()] * PREPARED,
        scratch_shapes=[pltpu.VMEM((3, tok * SUB, LANES), F32), scratch],
        compiler_params=params(60),
        cost_estimate=pl.CostEstimate(flops=40_000_000, bytes_accessed=6_000_000, transcendentals=0),
        name="prepare",
    )(seq_lengths, streams, cotangent, conv_weight, rate_t, gain_t)
    moved, *prepared = lax.optimization_barrier((moved, *prepared))
    rows = shards * OWN
    plane = pltpu.VMEM((rows, LANES), F32)
    payload = pl.pallas_call(
        functools.partial(owner_kernel, total),
        out_shape=jax.ShapeDtypeStruct((rows, LANES), BF16),
        in_specs=[smem()] + [vmem()] * 4,
        out_specs=vmem(),
        scratch_shapes=[
            pltpu.VMEM((3 * REACH, shards, SUB, LANES), F32),
            pltpu.VMEM((3 * TAPS, SUB, LANES), F32),
        ]
        + [plane] * 8
        + [pltpu.VMEM((8 * SUB, LANES), F32)] * 2
        + [pltpu.VMEM((LANES, LANES), F32)],
        compiler_params=params(22),
        name="owner",
    )(seq_lengths, moved, conv_weight, rate_t, gain_t)
    fields = lax.all_to_all(
        payload.reshape(shards, OWN, LANES), "ctx", split_axis=0, concat_axis=0, tiled=True
    ).reshape(rows, LANES)
    planes = lax.axis_size("ch")
    partial = pl.pallas_call(
        norm_kernel,
        out_shape=jax.ShapeDtypeStruct((planes, SUB, LANES), F32),
        in_specs=[vmem()],
        out_specs=vmem(),
        compiler_params=params(60),
        name="norm",
    )(fields)
    squares = lax.all_to_all(partial, "ch", split_axis=0, concat_axis=0, tiled=True)
    output, stream_grads, weight_grad = pl.pallas_call(
        functools.partial(shard_kernel, total),
        out_shape=[
            jax.ShapeDtypeStruct((tok, chans), BF16),
            jax.ShapeDtypeStruct((3, tok, chans), BF16),
            jax.ShapeDtypeStruct((3, TAPS, chans), F32),
        ],
        in_specs=[smem()] + [pl.BlockSpec(memory_space=pl.ANY)] * (1 + PREPARED),
        out_specs=[vmem()] * 3,
        scratch_shapes=[pltpu.VMEM(x.shape, x.dtype) for x in (fields, *prepared)]
        + [
            pltpu.SemaphoreType.DMA((1 + PREPARED,)),
            pltpu.VMEM((3, (REACH + EDGE) * SUB, LANES), F32),
            pltpu.VMEM((LANES * SUB, LANES), F32),
            pltpu.VMEM((2, EDGE * SUB, LANES), F32),
            pltpu.VMEM((EDGE * SUB, LANES), F32),
            pltpu.VMEM((3, (tok + REACH) * SUB, LANES), F32),
            scratch,
            pltpu.VMEM((3, tok * SUB, LANES), F32),
        ],
        compiler_params=params(60),
        cost_estimate=pl.CostEstimate(flops=40_000_000, bytes_accessed=6_000_000, transcendentals=0),
        name="shard",
    )(seq_lengths, fields, *prepared)
    clipped = pl.pallas_call(
        clip_kernel,
        out_shape=jax.ShapeDtypeStruct(weight_grad.shape, F32),
        in_specs=[vmem()] * 2,
        out_specs=vmem(),
        compiler_params=params(60),
        name="clip",
    )(weight_grad, squares)
    return output, stream_grads, clipped


def solution(mesh):
    return jax.shard_map(
        body,
        mesh=mesh,
        in_specs=(
            P(None, "ctx", "ch"),
            P(),
            P(None, None, "ch"),
            P("ch", None),
            P("ch", None),
            P("ctx", "ch"),
        ),
        out_specs=(P("ctx", "ch"), P(None, "ctx", "ch"), P(None, None, "ch")),
        check_vma=False,
    )
```

```python
import functools

import jax
import jax.numpy as jnp
from jax import lax
from jax.experimental import pallas as pl
from jax.experimental.pallas import tpu as pltpu
from jax.sharding import PartitionSpec as P

F32 = jnp.float32
BF16 = jnp.bfloat16
TAPS = 7
REACH = TAPS - 1
TOK = 128
LANES = 128
OWN = 8
SUB = 8
GROUP = 64
TURNS = 4
PREPARED = 10
EDGE = 8
SPAN = 40

LEFT = LANES - 3 * REACH
RIGHT = 0
STATE = 18
MODES = 16
GRADS = STATE + 4 * MODES


def rounded(value):
    return value.astype(BF16).astype(F32)


def halves(value):
    high = value.astype(BF16)
    return high, (value - high.astype(F32)).astype(BF16)


def one_minus_exp(x):
    series = jnp.full_like(x, 1.0)
    for n in range(11, 1, -1):
        series = 1.0 - (x * F32(1.0 / n)) * series
    return x * series


def gains(rate, gain):
    return gain * jnp.sqrt(one_minus_exp(2.0 * rate))


def start_list(seq_ref):
    starts = [jnp.int32(0)]
    for n in range(seq_ref.shape[0]):
        starts.append(starts[-1] + seq_ref[n])
    return starts


def dot(a, b):
    return lax.dot_general(a, b, (((1,), (0,)), ((), ())), preferred_element_type=F32)


def dot_t(a, b):
    return lax.dot_general(a, b, (((1,), (1,)), ((), ())), preferred_element_type=F32)


def turn_kernel(streams, cotangent, out, held, turned, arrive, leave):
    wide = held.shape[3]
    owners = wide // OWN
    coming = []
    for n in range(TURNS):
        cols = pl.ds(n * wide, wide)
        coming.append(
            (
                pltpu.make_async_copy(streams.at[:, :, cols], held.at[n, 0:3], arrive.at[n, 0]),
                pltpu.make_async_copy(cotangent.at[:, cols], held.at[n, 3], arrive.at[n, 1]),
            )
        )
        for copy in coming[-1]:
            copy.start()
    going = []
    for n in range(TURNS):
        for copy in coming[n]:
            copy.wait()
        for pair in range(2):
            for k in range(wide // LANES):
                cols = pl.ds(k * LANES, LANES)
                a, b = [
                    held[n, 2 * pair + i, :, cols].astype(F32).T.reshape(LANES // OWN, OWN, TOK)
                    for i in (0, 1)
                ]
                rows = pl.ds(n * owners + k * (LANES // OWN), LANES // OWN)
                turned[rows, pl.ds(pair * 16, 16), :] = jnp.concatenate([a, b], axis=1).astype(BF16)
        some = pl.ds(n * owners, owners)
        going.append(pltpu.make_async_copy(turned.at[some], out.at[some], leave.at[n]))
        going[-1].start()
    for copy in going:
        copy.wait()


ROWS_OF = (0, 8, 16, 24)


def owner_kernel(
    total, seq, moved, weight, rate, gain, out, sh, wide, u, dz, kc, vc, zs, ds, pay, halos, fixf, fixb, prm
):
    blocks = moved.shape[0]
    index = lax.axis_index("ctx")
    starts = start_list(seq)
    starts[-1] = jnp.int32(total)
    nseq = seq.shape[0]
    lane = lax.broadcasted_iota(jnp.int32, (SUB, LANES), 1)

    chunk = pl.multiple_of((index // (LANES // OWN)) * LANES, LANES)
    back = lax.rem(LANES - lax.rem(index, LANES // OWN) * OWN, LANES)
    cols = pl.ds(chunk, LANES)
    prm[...] = jnp.zeros_like(prm)
    prm[0:MODES, :] = pltpu.roll(rate[:, cols], back, 1)
    prm[MODES : 2 * MODES, :] = pltpu.roll(gain[:, cols], back, 1)
    for i in range(3):
        prm[32 + 8 * i : 32 + 8 * i + TAPS, :] = weight[i, :, cols]
    prm[32:56, :] = pltpu.roll(prm[32:56, :], back, 1)
    own = prm[...].T[0:OWN, :]
    for i in range(3):
        for j in range(TAPS):
            f = 32 + 8 * i + j
            wide[i * TAPS + j] = jnp.broadcast_to(own[:, f : f + 1], (SUB, LANES))
    rate_rows = jnp.concatenate(
        [jnp.broadcast_to(own[:, m : m + 1], (SUB, LANES)) for m in range(MODES)], axis=0
    )
    gain_rows = jnp.concatenate(
        [
            jnp.broadcast_to(own[:, MODES + m : MODES + m + 1], (SUB, LANES))
            for m in range(MODES)
        ],
        axis=0,
    )
    coef_rows = gains(rate_rows, gain_rows)

    def filtering(b, now, before, since):
        done = []
        for i in range(3):
            x = now[ROWS_OF[i] : ROWS_OF[i] + 8]
            p = before[ROWS_OF[i] : ROWS_OF[i] + 8]
            acc = wide[i * TAPS] * x
            for j in range(1, TAPS):
                moved_x = pltpu.roll(jnp.where(lane >= LANES - j, p, x), j, 1)
                if since is not None:
                    moved_x = jnp.where(since >= j, moved_x, 0.0)
                sh[i * REACH + j - 1, b] = moved_x
                acc = acc + wide[i * TAPS + j] * moved_x
            done.append(acc)
        rows = pl.ds(pl.multiple_of(b * SUB, SUB), SUB)
        u[rows, :] = rounded(done[1] * done[2])
        dz[rows, :] = rounded(now[24:32] * done[0])
        kc[rows, :] = done[1]
        vc[rows, :] = done[2]

    def filter_group(n, _):
        b0 = n * GROUP
        held = [moved[jnp.maximum(b0 - 1, 0)].astype(F32)]
        held += [moved[b0 + g].astype(F32) for g in range(GROUP)]
        for g in range(GROUP):
            filtering(b0 + g, held[g + 1], held[g], None)
        return 0

    lax.fori_loop(0, blocks // GROUP, filter_group, 0)
    for s in starts[:-1]:
        for near in (0, 1):
            b = jnp.minimum(s // TOK + near, blocks - 1)
            place = b * TOK + lane
            since = jnp.zeros((SUB, LANES), jnp.int32)
            for other in starts[:-1]:
                since = jnp.where(other <= place, other, since)
            filtering(
                b,
                moved[b].astype(F32),
                moved[jnp.maximum(b - 1, 0)].astype(F32),
                place - since,
            )

    for n in range(nseq):
        b = starts[n] // TOK
        rows = pl.ds(pl.multiple_of(b * SUB, SUB), SUB)
        place = b * TOK + lane
        fixf[n * SUB : (n + 1) * SUB, :] = jnp.where(place >= starts[n], u[rows, :], 0.0)
        fixb[n * SUB : (n + 1) * SUB, :] = jnp.where(place < starts[n], dz[rows, :], 0.0)

    row = lax.broadcasted_iota(jnp.int32, (blocks, TOK), 0)
    col = lax.broadcasted_iota(jnp.int32, (blocks, TOK), 1)
    head = jnp.ones((blocks, TOK), F32)
    tail = jnp.ones((blocks, TOK), F32)
    spot = row * TOK + col
    for s in starts[:-1]:
        base = s - lax.rem(s, TOK)
        head = jnp.where((spot >= s) & (spot < base + TOK), 0.0, head)
        tail = jnp.where((spot < s) & (spot >= base), 0.0, tail)

    lag = col.astype(F32)
    ending = halves(jnp.exp(-rate_rows * (TOK - 1.0 - lag)))
    falling = jnp.exp(-rate_rows * lag)
    opening = halves(falling)
    lead_f = halves(coef_rows * jnp.exp(-rate_rows * (lag + 1.0)))
    lead_b = halves(coef_rows * jnp.exp(-rate_rows * (TOK - lag)))
    whole = jnp.exp(-rate_rows * TOK).T[0:1, :]
    taps = (coef_rows * falling).reshape(MODES, OWN, LANES).sum(axis=0)

    mine = lax.rem(col, OWN)
    ending = jnp.concatenate(ending, axis=1)
    opening = jnp.concatenate(opening, axis=1)
    end_f = jnp.zeros((blocks, LANES), F32)
    end_b = jnp.zeros((blocks, LANES), F32)
    for c in range(OWN):
        uc = (u[pl.ds(c, blocks, stride=OWN), :] * tail).astype(BF16)
        dc = (dz[pl.ds(c, blocks, stride=OWN), :] * head).astype(BF16)
        ef = dot_t(jnp.concatenate([uc, uc], axis=1), ending)
        eb = dot_t(jnp.concatenate([dc, dc], axis=1), opening)
        end_f = jnp.where(mine == c, ef, end_f)
        end_b = jnp.where(mine == c, eb, end_b)

    keep_f = head[:, TOK - 1 : TOK] * whole
    keep_b = keep_f
    step = 1
    while step < blocks:
        low = row >= step
        end_f = end_f + jnp.where(low, keep_f * pltpu.roll(end_f, step, 0), 0.0)
        keep_f = jnp.where(low, keep_f * pltpu.roll(keep_f, step, 0), 0.0)
        high = row < blocks - step
        end_b = end_b + jnp.where(high, keep_b * pltpu.roll(end_b, blocks - step, 0), 0.0)
        keep_b = jnp.where(high, keep_b * pltpu.roll(keep_b, blocks - step, 0), 0.0)
        step *= 2
    state_f = jnp.where(row >= 1, pltpu.roll(end_f, 1, 0), 0.0)
    state_b = jnp.where(row < blocks - 1, pltpu.roll(end_b, blocks - 1, 0), 0.0)
    sf = halves(state_f)
    sb = halves(state_b)

    zero = jnp.zeros((blocks, LANES), BF16)
    every = jnp.concatenate([sf[0], sf[1], sb[0], sb[1]], axis=1)
    pick_row = lax.broadcasted_iota(jnp.int32, (4 * LANES, LANES), 0)
    pick_col = lax.broadcasted_iota(jnp.int32, (4 * LANES, LANES), 1)
    target = STATE + (pick_row // LANES) * MODES + lax.rem(pick_row, LANES) // OWN
    lands = pick_col == target
    pick_mine = lax.rem(pick_row, OWN)
    for c in range(OWN):
        strip = jnp.broadcast_to(taps[c : c + 1, :], (LANES, LANES))
        strip = pltpu.roll(strip, 0, 1, stride=1, stride_axis=0)
        strip = jnp.where(col >= row, strip, 0.0)
        kern = halves(strip)
        nrek = halves(strip.T)
        of_c = mine == c
        uc = u[pl.ds(c, blocks, stride=OWN), :].astype(BF16)
        dc = dz[pl.ds(c, blocks, stride=OWN), :].astype(BF16)
        fh, fl = [jnp.where(of_c, x, zero) for x in sf]
        bh, bl = [jnp.where(of_c, x, zero) for x in sb]
        both = jnp.concatenate([uc, fh], axis=1)
        zc = dot(both, jnp.concatenate([kern[0], lead_f[0]], axis=0))
        zc = zc + dot(both, jnp.concatenate([kern[1], lead_f[1]], axis=0))
        zs[pl.ds(c, blocks, stride=OWN), :] = zc + dot(fl, lead_f[0])
        both = jnp.concatenate([dc, bh], axis=1)
        rc = dot(both, jnp.concatenate([nrek[0], lead_b[0]], axis=0))
        rc = rc + dot(both, jnp.concatenate([nrek[1], lead_b[1]], axis=0))
        ds[pl.ds(c, blocks, stride=OWN), :] = rc + dot(bl, lead_b[0])
        few = fixf[pl.ds(c, nseq, stride=OWN), :].astype(BF16)
        fixf[pl.ds(c, nseq, stride=OWN), :] = dot(few, kern[0]) + dot(few, kern[1])
        few = fixb[pl.ds(c, nseq, stride=OWN), :].astype(BF16)
        fixb[pl.ds(c, nseq, stride=OWN), :] = dot(few, nrek[0]) + dot(few, nrek[1])
        pick = jnp.where(lands & (pick_mine == c), 1.0, 0.0).astype(BF16)
        pay[pl.ds(c, blocks, stride=OWN), :] = dot(every, pick)
    for n in range(nseq):
        b = starts[n] // TOK
        rows = pl.ds(pl.multiple_of(b * SUB, SUB), SUB)
        place = b * TOK + lane
        fresh = (place >= starts[n]) & (place < starts[n + 1])
        zs[rows, :] = jnp.where(fresh, fixf[n * SUB : (n + 1) * SUB, :], zs[rows, :])
        if n > 0:
            fresh = (place >= starts[n - 1]) & (place < starts[n])
            ds[rows, :] = jnp.where(fresh, fixb[n * SUB : (n + 1) * SUB, :], ds[rows, :])

    def gradient_group(n, acc):
        acc = list(acc)
        for g in range(GROUP):
            b = n * GROUP + g
            rows = pl.ds(pl.multiple_of(b * SUB, SUB), SUB)
            now = moved[b].astype(F32)
            z = rounded(zs[rows, :])
            d = rounded(ds[rows, :])
            df = (now[24:32] * z, d * vc[rows, :], d * kc[rows, :])
            for i in range(3):
                f = i * TAPS
                acc[f] = acc[f] + df[i] * now[ROWS_OF[i] : ROWS_OF[i] + 8]
                for j in range(1, TAPS):
                    acc[f + j] = acc[f + j] + df[i] * sh[i * REACH + j - 1, b]
            halo = jnp.where(lane < REACH, df[0], 0.0)
            for i in (1, 2):
                part = pltpu.roll(df[i], i * REACH, 1)
                halo = jnp.where((lane >= i * REACH) & (lane < (i + 1) * REACH), part, halo)
            halos[rows, :] = halo
        return tuple(acc)

    acc = lax.fori_loop(
        0,
        blocks // GROUP,
        gradient_group,
        tuple(jnp.zeros((SUB, LANES), F32) for _ in range(3 * TAPS)),
    )
    grads = jnp.zeros((SUB, LANES), F32)
    for f in range(3 * TAPS):
        grads = jnp.where(lane == GRADS + f, jnp.sum(acc[f], axis=1, keepdims=True), grads)

    def finish_group(n, _):
        b0 = n * GROUP
        held = [moved[jnp.maximum(b0 - 1, 0)].astype(F32)]
        held += [moved[b0 + g].astype(F32) for g in range(GROUP - 1)]
        tiles = []
        for g in range(GROUP):
            b = b0 + g
            after = jnp.minimum(b + 1, blocks - 1)
            value = pay[pl.ds(pl.multiple_of(b * SUB, SUB), SUB), :] + grads
            value = value + halos[pl.ds(pl.multiple_of(after * SUB, SUB), SUB), :]
            for i in range(3):
                x = held[g][ROWS_OF[i] : ROWS_OF[i] + 8]
                first = LEFT + i * REACH
                x = x if i == 2 else pltpu.roll(x, first - (TOK - REACH) + LANES, 1)
                value = jnp.where((lane >= first) & (lane < first + REACH), x, value)
            tiles.append(value)
        for g in range(0, GROUP, 2):
            rows = pl.ds(pl.multiple_of((b0 + g) * SUB, 16), 16)
            out[rows, :] = jnp.concatenate(tiles[g : g + 2], axis=0).astype(BF16)
        return 0

    lax.fori_loop(0, blocks // GROUP, finish_group, 0)


def put(ref, t, value):
    ref[pl.ds(pl.multiple_of(t * SUB, SUB), SUB), :] = value


def at(ref, t):
    return ref[pl.ds(pl.multiple_of(t * SUB, SUB), SUB), :]


def put3(ref, i, t, value):
    ref[i, pl.ds(pl.multiple_of(t * SUB, SUB), SUB), :] = value


def at3(ref, i, t):
    return ref[i, pl.ds(pl.multiple_of(t * SUB, SUB), SUB), :]


def tile(ref, n):
    return ref[pl.ds(n * SUB, SUB), :]


def local_starts(total, seq):
    index = lax.axis_index("ctx")
    local = [s - index * TOK for s in start_list(seq)]
    local[-1] = total - index * TOK
    return local


def since(local, t):
    last = local[0]
    for s in local[1:]:
        last = jnp.where(s <= t, s, last)
    return t - last


def until(local, t):
    following = local[-1]
    for s in local[-2::-1]:
        following = jnp.where(s > t, s, following)
    return following - t


def near(local, t0, count):
    found = jnp.bool_(False)
    for s in local:
        found = found | ((s >= t0 - REACH) & (s < t0 + count + REACH + 1))
    return found


def added(terms):
    while len(terms) > 1:
        rest = terms[len(terms) // 2 * 2 :]
        terms = [a + b for a, b in zip(terms[0::2], terms[1::2])] + rest
    return terms[0]


def scanned(prm, state, value, alive):
    for m in range(MODES):
        old = state[m]
        if alive is not None:
            old = jnp.where(alive, old, 0.0)
        state[m] = tile(prm, m) * old + value
    return added([tile(prm, MODES + m) * state[m] for m in range(MODES)])


def carried(prm, state, alive):
    for m in range(MODES):
        old = state[m]
        if alive is not None:
            old = jnp.where(alive, old, 0.0)
        state[m] = tile(prm, m) * old
    return added(list(state))


def eight_filtered(local, xs, ws, base, t0, masked):
    ages = [since(local, t0 + r) for r in range(8)] if masked else None
    done = []
    for i in range(3):
        w = [tile(ws, i * 8 + j) for j in range(TAPS)]
        x = [at3(xs, i, t0 + base - REACH + n) for n in range(8 + REACH)]
        row = []
        for r in range(8):
            acc = w[0] * x[r + REACH]
            for j in range(1, TAPS):
                term = w[j] * x[r + REACH - j]
                if masked:
                    term = jnp.where(ages[r] >= j, term, 0.0)
                acc = acc + term
            row.append(acc)
        done.append(row)
    return done


def prepare_kernel(
    total, seq, streams, cotangent, weight, rate, gain,
    heads, ws, prm, qs, zl, cots, ks, vs, dl, rl, xs, dzs,
):
    local = local_starts(total, seq)
    for k in range(SUB):
        cols = pl.ds(k * LANES, LANES)
        for g in range(MODES // 8):
            r = rate[g * 8 : g * 8 + 8, cols]
            prm[pl.ds(g * 64 + k, 8, stride=SUB), :] = jnp.exp(-r)
            prm[pl.ds(MODES * SUB + g * 64 + k, 8, stride=SUB), :] = gains(
                r, gain[g * 8 : g * 8 + 8, cols]
            )
        for i in range(3):
            ws[pl.ds(i * 64 + k, TAPS, stride=SUB), :] = weight[i, :, cols]
        for g in range(TOK // 16):
            some = pl.ds(g * 16, 16)
            for i in range(4):
                x = streams[i, some, cols] if i < 3 else cotangent[some, cols]
                x = x.astype(F32)
                for h in range(2):
                    rows = pl.ds((g * 16 + h * 8) * SUB + k, 8, stride=SUB)
                    part = x[h * 8 : h * 8 + 8]
                    if i == 3:
                        cots[rows, :] = part
                    else:
                        xs[i, rows, :] = part
                        if g == 0 and h == 0:
                            heads[i, rows, :] = part
    for ref in (qs, ks, vs, zl, dl):
        ref[0 : EDGE * SUB, :] = jnp.zeros((EDGE * SUB, LANES), F32)

    def forward(t0, state, masked):
        done = eight_filtered(local, xs, ws, 0, t0, masked)
        state = list(state)
        for r in range(8):
            t = t0 + r
            q, k, v = done[0][r], done[1][r], done[2][r]
            put(qs, t, q)
            put(ks, t, k)
            put(vs, t, v)
            put(dzs, t, rounded(at(cots, t) * q))
            alive = since(local, t) > 0 if masked else None
            put(zl, t, scanned(prm, state, rounded(k * v), alive))
        return tuple(state)

    def backward(t0, state, masked):
        state = list(state)
        for r in range(7, -1, -1):
            t = t0 + r
            alive = until(local, t) > 1 if masked else None
            put(dl, t, scanned(prm, state, at(dzs, t), alive))
        return tuple(state)

    def either(kernel, t0, state):
        return lax.cond(
            near(local, t0, 8),
            lambda s: kernel(t0, s, True),
            lambda s: kernel(t0, s, False),
            state,
        )

    zeros = tuple(jnp.zeros((SUB, LANES), F32) for _ in range(MODES))
    steps = (TOK - EDGE) // 8
    lax.fori_loop(0, steps, lambda n, s: either(forward, EDGE + n * 8, s), zeros)
    state = lax.fori_loop(0, steps, lambda n, s: either(backward, TOK - 8 - n * 8, s), zeros)
    for m in range(MODES):
        put(rl, m, state[m])


def shard_kernel(total, seq, *refs):
    far, refs = refs[: 1 + PREPARED], refs[1 + PREPARED :]
    out, grads_out, wgrad, *refs = refs
    held, refs = refs[: 1 + PREPARED], refs[1 + PREPARED :]
    arrive, leave, out_held, grads_held, wgrad_held, first, fs, q0, dz0, dfs, outs, sgs = refs
    fields, heads, ws, prm, qs, zl, cots, ks, vs, dl, rl = held
    coming = [None] + [
        pltpu.make_async_copy(far[n], held[n], arrive.at[n]) for n in range(1, 1 + PREPARED)
    ]
    halves_in = [
        pltpu.make_async_copy(
            far[0].at[pl.ds(h * 512, 512)], held[0].at[pl.ds(h * 512, 512)], arrive.at[h * (1 + PREPARED)]
        )
        for h in (0, 1)
    ]
    for copy in halves_in:
        copy.start()
    local = local_starts(total, seq)
    for k in range(SUB):
        if k == 0:
            halves_in[0].wait()
        if k == SUB // 2:
            halves_in[1].wait()
            for copy in coming[1:7]:
                copy.start()
        turned = fields[pl.ds(k * LANES, LANES), :].astype(F32).T
        for g in range(LANES // 8):
            fs[pl.ds(g * 64 + k, 8, stride=SUB), :] = turned[g * 8 : g * 8 + 8]
    for copy in coming[1:7]:
        copy.wait()
    for copy in coming[7:]:
        copy.start()
    for i in range(3):
        first[i, 0 : REACH * SUB, :] = fs[(LEFT + i * REACH) * SUB : (LEFT + (i + 1) * REACH) * SUB, :]
        first[i, REACH * SUB : (REACH + EDGE) * SUB, :] = heads[i]
        dfs[i, TOK * SUB : (TOK + REACH) * SUB, :] = fs[
            (RIGHT + i * REACH) * SUB : (RIGHT + (i + 1) * REACH) * SUB, :
        ]

    def entering(g):
        return [
            tile(fs, STATE + g * MODES + m) + tile(fs, STATE + (g + 1) * MODES + m)
            for m in range(MODES)
        ]

    def settle(t, q, z):
        z = rounded(z)
        put(outs, t, q * z)
        put3(dfs, 0, t, at(cots, t) * z)

    def settle_back(t, k, v, d):
        d = rounded(d)
        put3(dfs, 1, t, d * v)
        put3(dfs, 2, t, d * k)

    def adjoint(t0, count, masked):
        gaps = [until(local, t0 + r) for r in range(count)] if masked else None
        for i in range(3):
            w = [tile(ws, i * 8 + j) for j in range(TAPS)]
            y = [at3(dfs, i, t0 + n) for n in range(count + REACH)]
            for r in range(count):
                acc = w[0] * y[r]
                for j in range(1, TAPS):
                    term = w[j] * y[r + j]
                    if masked:
                        term = jnp.where(gaps[r] > j, term, 0.0)
                    acc = acc + term
                put3(sgs, i, t0 + r, acc)

    def forward(t0, state, masked):
        state = list(state)
        for r in range(SPAN):
            t = t0 + r
            alive = since(local, t) > 0 if masked else None
            settle(t, at(qs, t), at(zl, t) + carried(prm, state, alive))
        return tuple(state)

    def backward(t0, state, masked):
        state = list(state)
        for r in range(SPAN - 1, -1, -1):
            t = t0 + r
            alive = until(local, t) > 1 if masked else None
            settle_back(t, at(ks, t), at(vs, t), at(dl, t) + carried(prm, state, alive))
        adjoint(t0, SPAN, masked)
        return tuple(state)

    def either(kernel, t0, state):
        return lax.cond(
            near(local, t0, SPAN),
            lambda s: kernel(t0, s, True),
            lambda s: kernel(t0, s, False),
            state,
        )

    def weighted(state):
        return tuple(tile(prm, MODES + m) * state[m] for m in range(MODES))

    done = eight_filtered(local, first, ws, REACH, 0, True)
    state = entering(0)
    for t in range(EDGE):
        q, k, v = done[0][t], done[1][t], done[2][t]
        put(dz0, t, rounded(at(cots, t) * q))
        put3(q0, 0, t, k)
        put3(q0, 1, t, v)
        settle(t, q, scanned(prm, state, rounded(k * v), since(local, t) > 0))
    steps = (TOK - EDGE) // SPAN
    lax.fori_loop(0, steps, lambda n, s: either(forward, EDGE + n * SPAN, s), weighted(state))

    def finished(rows_of, target):
        for k in range(SUB):
            for g in range(TOK // 16):
                both = jnp.concatenate(
                    [rows_of(pl.ds((g * 16 + h * 8) * SUB + k, 8, stride=SUB)) for h in (0, 1)],
                    axis=0,
                )
                target[pl.ds(g * 16, 16), pl.ds(k * LANES, LANES)] = both.astype(BF16)

    for k in range(SUB):
        for i in range(3):
            wgrad_held[i, :, pl.ds(k * LANES, LANES)] = fs[
                pl.ds((GRADS + i * TAPS) * SUB + k, TAPS, stride=SUB), :
            ]
    finished(lambda rows: outs[rows, :], out_held)
    going = [
        pltpu.make_async_copy(wgrad_held, wgrad, leave.at[3]),
        pltpu.make_async_copy(out_held, out, leave.at[4]),
    ]
    for copy in going:
        copy.start()
    for copy in coming[7:]:
        copy.wait()
    carry = lax.fori_loop(
        0,
        steps,
        lambda n, s: either(backward, TOK - (n + 1) * SPAN, s),
        weighted(entering(2)),
    )
    carry = list(carry)
    state = [tile(rl, m) for m in range(MODES)]
    for t in range(EDGE - 1, -1, -1):
        alive = until(local, t) > 1
        d = scanned(prm, state, at(dz0, t), alive) + carried(prm, carry, alive)
        settle_back(t, at3(q0, 0, t), at3(q0, 1, t), d)
    adjoint(0, EDGE, True)

    for i in range(3):
        finished(lambda rows: sgs[i, rows, :], grads_held.at[i])
        going.append(pltpu.make_async_copy(grads_held.at[i], grads_out.at[i], leave.at[i]))
        going[-1].start()
    for copy in going:
        copy.wait()


def norm_kernel(fields, out):
    lane = lax.broadcasted_iota(jnp.int32, fields.shape, 1)
    value = fields[...].astype(F32)
    value = jnp.where((lane >= GRADS) & (lane < GRADS + 3 * TAPS), value, 0.0)
    out[...] = jnp.broadcast_to(jnp.sum(value * value), out.shape)


def clip_kernel(grads, squares, out):
    total = squares[0]
    for n in range(1, squares.shape[0]):
        total = total + squares[n]
    factor = jnp.minimum(F32(1.0), 1.0 / jnp.sqrt(total[0:1, :] + 1e-06))
    for k in range(grads.shape[2] // LANES):
        cols = pl.ds(k * LANES, LANES)
        for i in range(grads.shape[0]):
            out[i, :, cols] = grads[i, :, cols] * factor


def params(mebibytes):
    return pltpu.CompilerParams(vmem_limit_bytes=mebibytes * 1024 * 1024)


def vmem():
    return pl.BlockSpec(memory_space=pltpu.VMEM)


def smem():
    return pl.BlockSpec(memory_space=pltpu.SMEM)


def body(streams, seq_lengths, conv_weight, rate, modal_gain, cotangent):
    tok, chans = streams.shape[1:]
    shards = lax.axis_size("ctx")
    total = tok * shards
    rate_t, gain_t = rate.T, modal_gain.T
    turned = pl.pallas_call(
        turn_kernel,
        out_shape=jax.ShapeDtypeStruct((shards, 4 * OWN, tok), BF16),
        in_specs=[pl.BlockSpec(memory_space=pl.ANY)] * 2,
        out_specs=pl.BlockSpec(memory_space=pl.ANY),
        scratch_shapes=[
            pltpu.VMEM((TURNS, 4, tok, chans // TURNS), BF16),
            pltpu.VMEM((shards, 4 * OWN, tok), BF16),
            pltpu.SemaphoreType.DMA((TURNS, 2)),
            pltpu.SemaphoreType.DMA((TURNS,)),
        ],
        compiler_params=params(60),
        name="turn",
    )(streams, cotangent)
    moved = lax.all_to_all(turned, "ctx", split_axis=0, concat_axis=0, tiled=True)
    plane = jax.ShapeDtypeStruct((tok * SUB, LANES), F32)
    scratch = pltpu.VMEM((tok * SUB, LANES), F32)
    prepared = pl.pallas_call(
        functools.partial(prepare_kernel, total),
        out_shape=[
            jax.ShapeDtypeStruct((3, EDGE * SUB, LANES), F32),
            jax.ShapeDtypeStruct((3 * 8 * SUB, LANES), F32),
            jax.ShapeDtypeStruct((2 * MODES * SUB, LANES), F32),
        ]
        + [plane] * 6
        + [jax.ShapeDtypeStruct((MODES * SUB, LANES), F32)],
        in_specs=[smem()] + [vmem()] * 5,
        out_specs=[vmem()] * PREPARED,
        scratch_shapes=[pltpu.VMEM((3, tok * SUB, LANES), F32), scratch],
        compiler_params=params(60),
        cost_estimate=pl.CostEstimate(flops=40_000_000, bytes_accessed=6_000_000, transcendentals=0),
        name="prepare",
    )(seq_lengths, streams, cotangent, conv_weight, rate_t, gain_t)
    moved, *prepared = lax.optimization_barrier((moved, *prepared))
    rows = shards * OWN
    plane = pltpu.VMEM((rows, LANES), F32)
    payload = pl.pallas_call(
        functools.partial(owner_kernel, total),
        out_shape=jax.ShapeDtypeStruct((rows, LANES), BF16),
        in_specs=[smem()] + [vmem()] * 4,
        out_specs=vmem(),
        scratch_shapes=[
            pltpu.VMEM((3 * REACH, shards, SUB, LANES), F32),
            pltpu.VMEM((3 * TAPS, SUB, LANES), F32),
        ]
        + [plane] * 8
        + [pltpu.VMEM((8 * SUB, LANES), F32)] * 2
        + [pltpu.VMEM((LANES, LANES), F32)],
        compiler_params=params(22),
        name="owner",
    )(seq_lengths, moved, conv_weight, rate_t, gain_t)
    fields = lax.all_to_all(
        payload.reshape(shards, OWN, LANES), "ctx", split_axis=0, concat_axis=0, tiled=True
    ).reshape(rows, LANES)
    planes = lax.axis_size("ch")
    partial = pl.pallas_call(
        norm_kernel,
        out_shape=jax.ShapeDtypeStruct((planes, SUB, LANES), F32),
        in_specs=[vmem()],
        out_specs=vmem(),
        compiler_params=params(60),
        name="norm",
    )(fields)
    squares = lax.all_to_all(partial, "ch", split_axis=0, concat_axis=0, tiled=True)
    output, stream_grads, weight_grad = pl.pallas_call(
        functools.partial(shard_kernel, total),
        out_shape=[
            jax.ShapeDtypeStruct((tok, chans), BF16),
            jax.ShapeDtypeStruct((3, tok, chans), BF16),
            jax.ShapeDtypeStruct((3, TAPS, chans), F32),
        ],
        in_specs=[smem()] + [pl.BlockSpec(memory_space=pl.ANY)] * (1 + PREPARED),
        out_specs=[pl.BlockSpec(memory_space=pl.ANY)] * 3,
        scratch_shapes=[pltpu.VMEM(x.shape, x.dtype) for x in (fields, *prepared)]
        + [
            pltpu.SemaphoreType.DMA((2 + PREPARED,)),
            pltpu.SemaphoreType.DMA((5,)),
            pltpu.VMEM((tok, chans), BF16),
            pltpu.VMEM((3, tok, chans), BF16),
            pltpu.VMEM((3, TAPS, chans), F32),
            pltpu.VMEM((3, (REACH + EDGE) * SUB, LANES), F32),
            pltpu.VMEM((LANES * SUB, LANES), F32),
            pltpu.VMEM((2, EDGE * SUB, LANES), F32),
            pltpu.VMEM((EDGE * SUB, LANES), F32),
            pltpu.VMEM((3, (tok + REACH) * SUB, LANES), F32),
            scratch,
            pltpu.VMEM((3, tok * SUB, LANES), F32),
        ],
        compiler_params=params(60),
        cost_estimate=pl.CostEstimate(flops=40_000_000, bytes_accessed=6_000_000, transcendentals=0),
        name="shard",
    )(seq_lengths, fields, *prepared)
    clipped = pl.pallas_call(
        clip_kernel,
        out_shape=jax.ShapeDtypeStruct(weight_grad.shape, F32),
        in_specs=[vmem()] * 2,
        out_specs=vmem(),
        compiler_params=params(60),
        name="clip",
    )(weight_grad, squares)
    return output, stream_grads, clipped


def solution(mesh):
    return jax.shard_map(
        body,
        mesh=mesh,
        in_specs=(
            P(None, "ctx", "ch"),
            P(),
            P(None, None, "ch"),
            P("ch", None),
            P("ch", None),
            P("ctx", "ch"),
        ),
        out_specs=(P("ctx", "ch"), P(None, "ctx", "ch"), P(None, None, "ch")),
        check_vma=False,
    )
```

```python
import functools

import jax
import jax.numpy as jnp
from jax import lax
from jax.experimental import pallas as pl
from jax.experimental.pallas import tpu as pltpu
from jax.sharding import PartitionSpec as P

F32 = jnp.float32
BF16 = jnp.bfloat16
TAPS = 7
REACH = TAPS - 1
TOK = 128
LANES = 128
OWN = 8
SUB = 8
GROUP = 64
TURNS = 4
PREPARED = 10
EDGE = 8
SPAN = 40

LEFT = LANES - 3 * REACH
RIGHT = 0
STATE = 18
MODES = 16
GRADS = STATE + 4 * MODES


def rounded(value):
    return value.astype(BF16).astype(F32)


def halves(value):
    high = value.astype(BF16)
    return high, (value - high.astype(F32)).astype(BF16)


def one_minus_exp(x):
    series = jnp.full_like(x, 1.0)
    for n in range(11, 1, -1):
        series = 1.0 - (x * F32(1.0 / n)) * series
    return x * series


def gains(rate, gain):
    return gain * jnp.sqrt(one_minus_exp(2.0 * rate))


def start_list(seq_ref):
    starts = [jnp.int32(0)]
    for n in range(seq_ref.shape[0]):
        starts.append(starts[-1] + seq_ref[n])
    return starts


def dot(a, b):
    return lax.dot_general(a, b, (((1,), (0,)), ((), ())), preferred_element_type=F32)


def dot_t(a, b):
    return lax.dot_general(a, b, (((1,), (1,)), ((), ())), preferred_element_type=F32)


def turn_kernel(streams, cotangent, out, held, turned, arrive, leave):
    wide = held.shape[3]
    owners = wide // OWN
    coming = []
    for n in range(TURNS):
        cols = pl.ds(n * wide, wide)
        coming.append(
            (
                pltpu.make_async_copy(streams.at[:, :, cols], held.at[n, 0:3], arrive.at[n, 0]),
                pltpu.make_async_copy(cotangent.at[:, cols], held.at[n, 3], arrive.at[n, 1]),
            )
        )
        for copy in coming[-1]:
            copy.start()
    going = []
    for n in range(TURNS):
        for copy in coming[n]:
            copy.wait()
        for pair in range(2):
            for k in range(wide // LANES):
                cols = pl.ds(k * LANES, LANES)
                a, b = [
                    held[n, 2 * pair + i, :, cols].astype(F32).T.reshape(LANES // OWN, OWN, TOK)
                    for i in (0, 1)
                ]
                rows = pl.ds(n * owners + k * (LANES // OWN), LANES // OWN)
                turned[rows, pl.ds(pair * 16, 16), :] = jnp.concatenate([a, b], axis=1).astype(BF16)
        some = pl.ds(n * owners, owners)
        going.append(pltpu.make_async_copy(turned.at[some], out.at[some], leave.at[n]))
        going[-1].start()
    for copy in going:
        copy.wait()


ROWS_OF = (0, 8, 16, 24)


def owner_kernel(
    total, seq, moved, weight, rate, gain, out, sh, wide, u, dz, kc, vc, zs, ds, pay, halos, fixf, fixb, prm
):
    blocks = moved.shape[0]
    index = lax.axis_index("ctx")
    starts = start_list(seq)
    starts[-1] = jnp.int32(total)
    nseq = seq.shape[0]
    lane = lax.broadcasted_iota(jnp.int32, (SUB, LANES), 1)

    chunk = pl.multiple_of((index // (LANES // OWN)) * LANES, LANES)
    back = lax.rem(LANES - lax.rem(index, LANES // OWN) * OWN, LANES)
    cols = pl.ds(chunk, LANES)
    prm[...] = jnp.zeros_like(prm)
    prm[0:MODES, :] = pltpu.roll(rate[:, cols], back, 1)
    prm[MODES : 2 * MODES, :] = pltpu.roll(gain[:, cols], back, 1)
    for i in range(3):
        prm[32 + 8 * i : 32 + 8 * i + TAPS, :] = weight[i, :, cols]
    prm[32:56, :] = pltpu.roll(prm[32:56, :], back, 1)
    own = prm[...].T[0:OWN, :]
    for i in range(3):
        for j in range(TAPS):
            f = 32 + 8 * i + j
            wide[i * TAPS + j] = jnp.broadcast_to(own[:, f : f + 1], (SUB, LANES))
    rate_rows = jnp.concatenate(
        [jnp.broadcast_to(own[:, m : m + 1], (SUB, LANES)) for m in range(MODES)], axis=0
    )
    gain_rows = jnp.concatenate(
        [
            jnp.broadcast_to(own[:, MODES + m : MODES + m + 1], (SUB, LANES))
            for m in range(MODES)
        ],
        axis=0,
    )
    coef_rows = gains(rate_rows, gain_rows)

    def filtering(b, now, before, since):
        done = []
        for i in range(3):
            x = now[ROWS_OF[i] : ROWS_OF[i] + 8]
            p = before[ROWS_OF[i] : ROWS_OF[i] + 8]
            acc = wide[i * TAPS] * x
            for j in range(1, TAPS):
                moved_x = pltpu.roll(jnp.where(lane >= LANES - j, p, x), j, 1)
                if since is not None:
                    moved_x = jnp.where(since >= j, moved_x, 0.0)
                sh[i * REACH + j - 1, b] = moved_x
                acc = acc + wide[i * TAPS + j] * moved_x
            done.append(acc)
        rows = pl.ds(pl.multiple_of(b * SUB, SUB), SUB)
        u[rows, :] = rounded(done[1] * done[2])
        dz[rows, :] = rounded(now[24:32] * done[0])
        kc[rows, :] = done[1]
        vc[rows, :] = done[2]

    def filter_group(n, _):
        b0 = n * GROUP
        held = [moved[jnp.maximum(b0 - 1, 0)].astype(F32)]
        held += [moved[b0 + g].astype(F32) for g in range(GROUP)]
        for g in range(GROUP):
            filtering(b0 + g, held[g + 1], held[g], None)
        return 0

    lax.fori_loop(0, blocks // GROUP, filter_group, 0)
    for s in starts[:-1]:
        for near in (0, 1):
            b = jnp.minimum(s // TOK + near, blocks - 1)
            place = b * TOK + lane
            since = jnp.zeros((SUB, LANES), jnp.int32)
            for other in starts[:-1]:
                since = jnp.where(other <= place, other, since)
            filtering(
                b,
                moved[b].astype(F32),
                moved[jnp.maximum(b - 1, 0)].astype(F32),
                place - since,
            )

    for n in range(nseq):
        b = starts[n] // TOK
        rows = pl.ds(pl.multiple_of(b * SUB, SUB), SUB)
        place = b * TOK + lane
        fixf[n * SUB : (n + 1) * SUB, :] = jnp.where(place >= starts[n], u[rows, :], 0.0)
        fixb[n * SUB : (n + 1) * SUB, :] = jnp.where(place < starts[n], dz[rows, :], 0.0)

    row = lax.broadcasted_iota(jnp.int32, (blocks, TOK), 0)
    col = lax.broadcasted_iota(jnp.int32, (blocks, TOK), 1)
    head = jnp.ones((blocks, TOK), F32)
    tail = jnp.ones((blocks, TOK), F32)
    spot = row * TOK + col
    for s in starts[:-1]:
        base = s - lax.rem(s, TOK)
        head = jnp.where((spot >= s) & (spot < base + TOK), 0.0, head)
        tail = jnp.where((spot < s) & (spot >= base), 0.0, tail)

    lag = col.astype(F32)
    ending = halves(jnp.exp(-rate_rows * (TOK - 1.0 - lag)))
    falling = jnp.exp(-rate_rows * lag)
    opening = halves(falling)
    lead_f = halves(coef_rows * jnp.exp(-rate_rows * (lag + 1.0)))
    lead_b = halves(coef_rows * jnp.exp(-rate_rows * (TOK - lag)))
    whole = jnp.exp(-rate_rows * TOK).T[0:1, :]
    taps = (coef_rows * falling).reshape(MODES, OWN, LANES).sum(axis=0)

    mine = lax.rem(col, OWN)
    ending = jnp.concatenate(ending, axis=1)
    opening = jnp.concatenate(opening, axis=1)
    end_f = jnp.zeros((blocks, LANES), F32)
    end_b = jnp.zeros((blocks, LANES), F32)
    for c in range(OWN):
        uc = (u[pl.ds(c, blocks, stride=OWN), :] * tail).astype(BF16)
        dc = (dz[pl.ds(c, blocks, stride=OWN), :] * head).astype(BF16)
        ef = dot_t(jnp.concatenate([uc, uc], axis=1), ending)
        eb = dot_t(jnp.concatenate([dc, dc], axis=1), opening)
        end_f = jnp.where(mine == c, ef, end_f)
        end_b = jnp.where(mine == c, eb, end_b)

    keep_f = head[:, TOK - 1 : TOK] * whole
    keep_b = keep_f
    step = 1
    while step < blocks:
        low = row >= step
        end_f = end_f + jnp.where(low, keep_f * pltpu.roll(end_f, step, 0), 0.0)
        keep_f = jnp.where(low, keep_f * pltpu.roll(keep_f, step, 0), 0.0)
        high = row < blocks - step
        end_b = end_b + jnp.where(high, keep_b * pltpu.roll(end_b, blocks - step, 0), 0.0)
        keep_b = jnp.where(high, keep_b * pltpu.roll(keep_b, blocks - step, 0), 0.0)
        step *= 2
    state_f = jnp.where(row >= 1, pltpu.roll(end_f, 1, 0), 0.0)
    state_b = jnp.where(row < blocks - 1, pltpu.roll(end_b, blocks - 1, 0), 0.0)
    sf = halves(state_f)
    sb = halves(state_b)

    zero = jnp.zeros((blocks, LANES), BF16)
    every = jnp.concatenate([sf[0], sf[1], sb[0], sb[1]], axis=1)
    pick_row = lax.broadcasted_iota(jnp.int32, (4 * LANES, LANES), 0)
    pick_col = lax.broadcasted_iota(jnp.int32, (4 * LANES, LANES), 1)
    target = STATE + (pick_row // LANES) * MODES + lax.rem(pick_row, LANES) // OWN
    lands = pick_col == target
    pick_mine = lax.rem(pick_row, OWN)
    for c in range(OWN):
        strip = jnp.broadcast_to(taps[c : c + 1, :], (LANES, LANES))
        strip = pltpu.roll(strip, 0, 1, stride=1, stride_axis=0)
        strip = jnp.where(col >= row, strip, 0.0)
        kern = halves(strip)
        nrek = halves(strip.T)
        of_c = mine == c
        uc = u[pl.ds(c, blocks, stride=OWN), :].astype(BF16)
        dc = dz[pl.ds(c, blocks, stride=OWN), :].astype(BF16)
        fh, fl = [jnp.where(of_c, x, zero) for x in sf]
        bh, bl = [jnp.where(of_c, x, zero) for x in sb]
        both = jnp.concatenate([uc, fh], axis=1)
        zc = dot(both, jnp.concatenate([kern[0], lead_f[0]], axis=0))
        zc = zc + dot(both, jnp.concatenate([kern[1], lead_f[1]], axis=0))
        zs[pl.ds(c, blocks, stride=OWN), :] = zc + dot(fl, lead_f[0])
        both = jnp.concatenate([dc, bh], axis=1)
        rc = dot(both, jnp.concatenate([nrek[0], lead_b[0]], axis=0))
        rc = rc + dot(both, jnp.concatenate([nrek[1], lead_b[1]], axis=0))
        ds[pl.ds(c, blocks, stride=OWN), :] = rc + dot(bl, lead_b[0])
        few = fixf[pl.ds(c, nseq, stride=OWN), :].astype(BF16)
        fixf[pl.ds(c, nseq, stride=OWN), :] = dot(few, kern[0]) + dot(few, kern[1])
        few = fixb[pl.ds(c, nseq, stride=OWN), :].astype(BF16)
        fixb[pl.ds(c, nseq, stride=OWN), :] = dot(few, nrek[0]) + dot(few, nrek[1])
        pick = jnp.where(lands & (pick_mine == c), 1.0, 0.0).astype(BF16)
        pay[pl.ds(c, blocks, stride=OWN), :] = dot(every, pick)
    for n in range(nseq):
        b = starts[n] // TOK
        rows = pl.ds(pl.multiple_of(b * SUB, SUB), SUB)
        place = b * TOK + lane
        fresh = (place >= starts[n]) & (place < starts[n + 1])
        zs[rows, :] = jnp.where(fresh, fixf[n * SUB : (n + 1) * SUB, :], zs[rows, :])
        if n > 0:
            fresh = (place >= starts[n - 1]) & (place < starts[n])
            ds[rows, :] = jnp.where(fresh, fixb[n * SUB : (n + 1) * SUB, :], ds[rows, :])

    def gradient_group(n, acc):
        acc = list(acc)
        for g in range(GROUP):
            b = n * GROUP + g
            rows = pl.ds(pl.multiple_of(b * SUB, SUB), SUB)
            now = moved[b].astype(F32)
            z = rounded(zs[rows, :])
            d = rounded(ds[rows, :])
            df = (now[24:32] * z, d * vc[rows, :], d * kc[rows, :])
            for i in range(3):
                f = i * TAPS
                acc[f] = acc[f] + df[i] * now[ROWS_OF[i] : ROWS_OF[i] + 8]
                for j in range(1, TAPS):
                    acc[f + j] = acc[f + j] + df[i] * sh[i * REACH + j - 1, b]
            halo = jnp.where(lane < REACH, df[0], 0.0)
            for i in (1, 2):
                part = pltpu.roll(df[i], i * REACH, 1)
                halo = jnp.where((lane >= i * REACH) & (lane < (i + 1) * REACH), part, halo)
            halos[rows, :] = halo
        return tuple(acc)

    acc = lax.fori_loop(
        0,
        blocks // GROUP,
        gradient_group,
        tuple(jnp.zeros((SUB, LANES), F32) for _ in range(3 * TAPS)),
    )
    grads = jnp.zeros((SUB, LANES), F32)
    for f in range(3 * TAPS):
        grads = jnp.where(lane == GRADS + f, jnp.sum(acc[f], axis=1, keepdims=True), grads)

    def finish_group(n, _):
        b0 = n * GROUP
        held = [moved[jnp.maximum(b0 - 1, 0)].astype(F32)]
        held += [moved[b0 + g].astype(F32) for g in range(GROUP - 1)]
        tiles = []
        for g in range(GROUP):
            b = b0 + g
            after = jnp.minimum(b + 1, blocks - 1)
            value = pay[pl.ds(pl.multiple_of(b * SUB, SUB), SUB), :] + grads
            value = value + halos[pl.ds(pl.multiple_of(after * SUB, SUB), SUB), :]
            for i in range(3):
                x = held[g][ROWS_OF[i] : ROWS_OF[i] + 8]
                first = LEFT + i * REACH
                x = x if i == 2 else pltpu.roll(x, first - (TOK - REACH) + LANES, 1)
                value = jnp.where((lane >= first) & (lane < first + REACH), x, value)
            tiles.append(value)
        for g in range(0, GROUP, 2):
            rows = pl.ds(pl.multiple_of((b0 + g) * SUB, 16), 16)
            out[rows, :] = jnp.concatenate(tiles[g : g + 2], axis=0).astype(BF16)
        return 0

    lax.fori_loop(0, blocks // GROUP, finish_group, 0)


def put(ref, t, value):
    ref[pl.ds(pl.multiple_of(t * SUB, SUB), SUB), :] = value


def at(ref, t):
    return ref[pl.ds(pl.multiple_of(t * SUB, SUB), SUB), :]


def put3(ref, i, t, value):
    ref[i, pl.ds(pl.multiple_of(t * SUB, SUB), SUB), :] = value


def at3(ref, i, t):
    return ref[i, pl.ds(pl.multiple_of(t * SUB, SUB), SUB), :]


def tile(ref, n):
    return ref[pl.ds(n * SUB, SUB), :]


def local_starts(total, seq):
    index = lax.axis_index("ctx")
    local = [s - index * TOK for s in start_list(seq)]
    local[-1] = total - index * TOK
    return local


def since(local, t):
    last = local[0]
    for s in local[1:]:
        last = jnp.where(s <= t, s, last)
    return t - last


def until(local, t):
    following = local[-1]
    for s in local[-2::-1]:
        following = jnp.where(s > t, s, following)
    return following - t


def near(local, t0, count):
    found = jnp.bool_(False)
    for s in local:
        found = found | ((s >= t0 - REACH) & (s < t0 + count + REACH + 1))
    return found


def added(terms):
    while len(terms) > 1:
        rest = terms[len(terms) // 2 * 2 :]
        terms = [a + b for a, b in zip(terms[0::2], terms[1::2])] + rest
    return terms[0]


def scanned(prm, state, value, alive):
    for m in range(MODES):
        old = state[m]
        if alive is not None:
            old = jnp.where(alive, old, 0.0)
        state[m] = tile(prm, m) * old + value
    return added([tile(prm, MODES + m) * state[m] for m in range(MODES)])


def carried(prm, state, alive):
    for m in range(MODES):
        old = state[m]
        if alive is not None:
            old = jnp.where(alive, old, 0.0)
        state[m] = tile(prm, m) * old
    return added(list(state))


def eight_filtered(local, xs, ws, base, t0, masked):
    ages = [since(local, t0 + r) for r in range(8)] if masked else None
    done = []
    for i in range(3):
        w = [tile(ws, i * 8 + j) for j in range(TAPS)]
        x = [at3(xs, i, t0 + base - REACH + n) for n in range(8 + REACH)]
        row = []
        for r in range(8):
            acc = w[0] * x[r + REACH]
            for j in range(1, TAPS):
                term = w[j] * x[r + REACH - j]
                if masked:
                    term = jnp.where(ages[r] >= j, term, 0.0)
                acc = acc + term
            row.append(acc)
        done.append(row)
    return done


def prepare_kernel(
    total, seq, streams, cotangent, weight, rate, gain,
    heads, ws, prm, qs, zl, cots, ks, vs, dl, rl, xs, dzs,
):
    local = local_starts(total, seq)
    for k in range(SUB):
        cols = pl.ds(k * LANES, LANES)
        for g in range(MODES // 8):
            r = rate[g * 8 : g * 8 + 8, cols]
            prm[pl.ds(g * 64 + k, 8, stride=SUB), :] = jnp.exp(-r)
            prm[pl.ds(MODES * SUB + g * 64 + k, 8, stride=SUB), :] = gains(
                r, gain[g * 8 : g * 8 + 8, cols]
            )
        for i in range(3):
            ws[pl.ds(i * 64 + k, TAPS, stride=SUB), :] = weight[i, :, cols]
        for g in range(TOK // 16):
            some = pl.ds(g * 16, 16)
            for i in range(4):
                x = streams[i, some, cols] if i < 3 else cotangent[some, cols]
                x = x.astype(F32)
                for h in range(2):
                    rows = pl.ds((g * 16 + h * 8) * SUB + k, 8, stride=SUB)
                    part = x[h * 8 : h * 8 + 8]
                    if i == 3:
                        cots[rows, :] = part
                    else:
                        xs[i, rows, :] = part
                        if g == 0 and h == 0:
                            heads[i, rows, :] = part
    for ref in (qs, ks, vs, zl, dl):
        ref[0 : EDGE * SUB, :] = jnp.zeros((EDGE * SUB, LANES), F32)

    def forward(t0, state, masked):
        done = eight_filtered(local, xs, ws, 0, t0, masked)
        state = list(state)
        for r in range(8):
            t = t0 + r
            q, k, v = done[0][r], done[1][r], done[2][r]
            put(qs, t, q)
            put(ks, t, k)
            put(vs, t, v)
            put(dzs, t, rounded(at(cots, t) * q))
            alive = since(local, t) > 0 if masked else None
            put(zl, t, scanned(prm, state, rounded(k * v), alive))
        return tuple(state)

    def backward(t0, state, masked):
        state = list(state)
        for r in range(7, -1, -1):
            t = t0 + r
            alive = until(local, t) > 1 if masked else None
            put(dl, t, scanned(prm, state, at(dzs, t), alive))
        return tuple(state)

    def either(kernel, t0, state):
        return lax.cond(
            near(local, t0, 8),
            lambda s: kernel(t0, s, True),
            lambda s: kernel(t0, s, False),
            state,
        )

    zeros = tuple(jnp.zeros((SUB, LANES), F32) for _ in range(MODES))
    steps = (TOK - EDGE) // 8
    lax.fori_loop(0, steps, lambda n, s: either(forward, EDGE + n * 8, s), zeros)
    state = lax.fori_loop(0, steps, lambda n, s: either(backward, TOK - 8 - n * 8, s), zeros)
    for m in range(MODES):
        put(rl, m, state[m])


def shard_kernel(total, seq, *refs):
    far, refs = refs[: 1 + PREPARED], refs[1 + PREPARED :]
    out, grads_out, wgrad, *refs = refs
    held, refs = refs[: 1 + PREPARED], refs[1 + PREPARED :]
    arrive, leave, out_held, grads_held, wgrad_held, first, fs, q0, dz0, dfs, outs, sgs = refs
    fields, heads, ws, prm, qs, zl, cots, ks, vs, dl, rl = held
    coming = []
    for n in range(1 + PREPARED):
        coming.append(pltpu.make_async_copy(far[n], held[n], arrive.at[n]))
        coming[-1].start()
    local = local_starts(total, seq)
    coming[0].wait()
    for k in range(SUB):
        cols = pl.ds(k * LANES, LANES)
        turned = fields[pl.ds(k * LANES, LANES), :].astype(F32).T
        for g in range(LANES // 8):
            fs[pl.ds(g * 64 + k, 8, stride=SUB), :] = turned[g * 8 : g * 8 + 8]
    for copy in coming[1:7]:
        copy.wait()
    for i in range(3):
        first[i, 0 : REACH * SUB, :] = fs[(LEFT + i * REACH) * SUB : (LEFT + (i + 1) * REACH) * SUB, :]
        first[i, REACH * SUB : (REACH + EDGE) * SUB, :] = heads[i]
        dfs[i, TOK * SUB : (TOK + REACH) * SUB, :] = fs[
            (RIGHT + i * REACH) * SUB : (RIGHT + (i + 1) * REACH) * SUB, :
        ]

    def entering(g):
        return [
            tile(fs, STATE + g * MODES + m) + tile(fs, STATE + (g + 1) * MODES + m)
            for m in range(MODES)
        ]

    def settle(t, q, z):
        z = rounded(z)
        put(outs, t, q * z)
        put3(dfs, 0, t, at(cots, t) * z)

    def settle_back(t, k, v, d):
        d = rounded(d)
        put3(dfs, 1, t, d * v)
        put3(dfs, 2, t, d * k)

    def adjoint(t0, count, masked):
        gaps = [until(local, t0 + r) for r in range(count)] if masked else None
        for i in range(3):
            w = [tile(ws, i * 8 + j) for j in range(TAPS)]
            y = [at3(dfs, i, t0 + n) for n in range(count + REACH)]
            for r in range(count):
                acc = w[0] * y[r]
                for j in range(1, TAPS):
                    term = w[j] * y[r + j]
                    if masked:
                        term = jnp.where(gaps[r] > j, term, 0.0)
                    acc = acc + term
                put3(sgs, i, t0 + r, acc)

    def forward(t0, state, masked):
        state = list(state)
        for r in range(SPAN):
            t = t0 + r
            alive = since(local, t) > 0 if masked else None
            settle(t, at(qs, t), at(zl, t) + carried(prm, state, alive))
        return tuple(state)

    def backward(t0, state, masked):
        state = list(state)
        for r in range(SPAN - 1, -1, -1):
            t = t0 + r
            alive = until(local, t) > 1 if masked else None
            settle_back(t, at(ks, t), at(vs, t), at(dl, t) + carried(prm, state, alive))
        adjoint(t0, SPAN, masked)
        return tuple(state)

    def either(kernel, t0, state):
        return lax.cond(
            near(local, t0, SPAN),
            lambda s: kernel(t0, s, True),
            lambda s: kernel(t0, s, False),
            state,
        )

    def weighted(state):
        return tuple(tile(prm, MODES + m) * state[m] for m in range(MODES))

    done = eight_filtered(local, first, ws, REACH, 0, True)
    state = entering(0)
    for t in range(EDGE):
        q, k, v = done[0][t], done[1][t], done[2][t]
        put(dz0, t, rounded(at(cots, t) * q))
        put3(q0, 0, t, k)
        put3(q0, 1, t, v)
        settle(t, q, scanned(prm, state, rounded(k * v), since(local, t) > 0))
    steps = (TOK - EDGE) // SPAN
    lax.fori_loop(0, steps, lambda n, s: either(forward, EDGE + n * SPAN, s), weighted(state))

    def finished(rows_of, target):
        for k in range(SUB):
            for g in range(TOK // 16):
                both = jnp.concatenate(
                    [rows_of(pl.ds((g * 16 + h * 8) * SUB + k, 8, stride=SUB)) for h in (0, 1)],
                    axis=0,
                )
                target[pl.ds(g * 16, 16), pl.ds(k * LANES, LANES)] = both.astype(BF16)

    for k in range(SUB):
        for i in range(3):
            wgrad_held[i, :, pl.ds(k * LANES, LANES)] = fs[
                pl.ds((GRADS + i * TAPS) * SUB + k, TAPS, stride=SUB), :
            ]
    finished(lambda rows: outs[rows, :], out_held)
    going = [
        pltpu.make_async_copy(wgrad_held, wgrad, leave.at[3]),
        pltpu.make_async_copy(out_held, out, leave.at[4]),
    ]
    for copy in going:
        copy.start()
    for copy in coming[7:]:
        copy.wait()
    carry = lax.fori_loop(
        0,
        steps,
        lambda n, s: either(backward, TOK - (n + 1) * SPAN, s),
        weighted(entering(2)),
    )
    carry = list(carry)
    state = [tile(rl, m) for m in range(MODES)]
    for t in range(EDGE - 1, -1, -1):
        alive = until(local, t) > 1
        d = scanned(prm, state, at(dz0, t), alive) + carried(prm, carry, alive)
        settle_back(t, at3(q0, 0, t), at3(q0, 1, t), d)
    adjoint(0, EDGE, True)

    for i in range(3):
        finished(lambda rows: sgs[i, rows, :], grads_held.at[i])
        going.append(pltpu.make_async_copy(grads_held.at[i], grads_out.at[i], leave.at[i]))
        going[-1].start()
    for copy in going:
        copy.wait()


def norm_kernel(fields, out):
    lane = lax.broadcasted_iota(jnp.int32, fields.shape, 1)
    value = fields[...].astype(F32)
    value = jnp.where((lane >= GRADS) & (lane < GRADS + 3 * TAPS), value, 0.0)
    out[...] = jnp.broadcast_to(jnp.sum(value * value), out.shape)


def clip_kernel(grads, squares, out):
    total = squares[0]
    for n in range(1, squares.shape[0]):
        total = total + squares[n]
    factor = jnp.minimum(F32(1.0), 1.0 / jnp.sqrt(total[0:1, :] + 1e-06))
    for k in range(grads.shape[2] // LANES):
        cols = pl.ds(k * LANES, LANES)
        for i in range(grads.shape[0]):
            out[i, :, cols] = grads[i, :, cols] * factor


def params(mebibytes):
    return pltpu.CompilerParams(vmem_limit_bytes=mebibytes * 1024 * 1024)


def vmem():
    return pl.BlockSpec(memory_space=pltpu.VMEM)


def smem():
    return pl.BlockSpec(memory_space=pltpu.SMEM)


def body(streams, seq_lengths, conv_weight, rate, modal_gain, cotangent):
    tok, chans = streams.shape[1:]
    shards = lax.axis_size("ctx")
    total = tok * shards
    rate_t, gain_t = rate.T, modal_gain.T
    turned = pl.pallas_call(
        turn_kernel,
        out_shape=jax.ShapeDtypeStruct((shards, 4 * OWN, tok), BF16),
        in_specs=[pl.BlockSpec(memory_space=pl.ANY)] * 2,
        out_specs=pl.BlockSpec(memory_space=pl.ANY),
        scratch_shapes=[
            pltpu.VMEM((TURNS, 4, tok, chans // TURNS), BF16),
            pltpu.VMEM((shards, 4 * OWN, tok), BF16),
            pltpu.SemaphoreType.DMA((TURNS, 2)),
            pltpu.SemaphoreType.DMA((TURNS,)),
        ],
        compiler_params=params(60),
        name="turn",
    )(streams, cotangent)
    moved = lax.all_to_all(turned, "ctx", split_axis=0, concat_axis=0, tiled=True)
    plane = jax.ShapeDtypeStruct((tok * SUB, LANES), F32)
    scratch = pltpu.VMEM((tok * SUB, LANES), F32)
    prepared = pl.pallas_call(
        functools.partial(prepare_kernel, total),
        out_shape=[
            jax.ShapeDtypeStruct((3, EDGE * SUB, LANES), F32),
            jax.ShapeDtypeStruct((3 * 8 * SUB, LANES), F32),
            jax.ShapeDtypeStruct((2 * MODES * SUB, LANES), F32),
        ]
        + [plane] * 6
        + [jax.ShapeDtypeStruct((MODES * SUB, LANES), F32)],
        in_specs=[smem()] + [vmem()] * 5,
        out_specs=[vmem()] * PREPARED,
        scratch_shapes=[pltpu.VMEM((3, tok * SUB, LANES), F32), scratch],
        compiler_params=params(60),
        cost_estimate=pl.CostEstimate(flops=40_000_000, bytes_accessed=6_000_000, transcendentals=0),
        name="prepare",
    )(seq_lengths, streams, cotangent, conv_weight, rate_t, gain_t)
    moved, *prepared = lax.optimization_barrier((moved, *prepared))
    rows = shards * OWN
    plane = pltpu.VMEM((rows, LANES), F32)
    payload = pl.pallas_call(
        functools.partial(owner_kernel, total),
        out_shape=jax.ShapeDtypeStruct((rows, LANES), BF16),
        in_specs=[smem()] + [vmem()] * 4,
        out_specs=vmem(),
        scratch_shapes=[
            pltpu.VMEM((3 * REACH, shards, SUB, LANES), F32),
            pltpu.VMEM((3 * TAPS, SUB, LANES), F32),
        ]
        + [plane] * 8
        + [pltpu.VMEM((8 * SUB, LANES), F32)] * 2
        + [pltpu.VMEM((LANES, LANES), F32)],
        compiler_params=params(22),
        name="owner",
    )(seq_lengths, moved, conv_weight, rate_t, gain_t)
    fields = lax.all_to_all(
        payload.reshape(shards, OWN, LANES), "ctx", split_axis=0, concat_axis=0, tiled=True
    ).reshape(rows, LANES)
    planes = lax.axis_size("ch")
    partial = pl.pallas_call(
        norm_kernel,
        out_shape=jax.ShapeDtypeStruct((planes, SUB, LANES), F32),
        in_specs=[vmem()],
        out_specs=vmem(),
        compiler_params=params(60),
        name="norm",
    )(fields)
    squares = lax.all_to_all(partial, "ch", split_axis=0, concat_axis=0, tiled=True)
    output, stream_grads, weight_grad = pl.pallas_call(
        functools.partial(shard_kernel, total),
        out_shape=[
            jax.ShapeDtypeStruct((tok, chans), BF16),
            jax.ShapeDtypeStruct((3, tok, chans), BF16),
            jax.ShapeDtypeStruct((3, TAPS, chans), F32),
        ],
        in_specs=[smem()] + [pl.BlockSpec(memory_space=pl.ANY)] * (1 + PREPARED),
        out_specs=[pl.BlockSpec(memory_space=pl.ANY)] * 3,
        scratch_shapes=[pltpu.VMEM(x.shape, x.dtype) for x in (fields, *prepared)]
        + [
            pltpu.SemaphoreType.DMA((1 + PREPARED,)),
            pltpu.SemaphoreType.DMA((5,)),
            pltpu.VMEM((tok, chans), BF16),
            pltpu.VMEM((3, tok, chans), BF16),
            pltpu.VMEM((3, TAPS, chans), F32),
            pltpu.VMEM((3, (REACH + EDGE) * SUB, LANES), F32),
            pltpu.VMEM((LANES * SUB, LANES), F32),
            pltpu.VMEM((2, EDGE * SUB, LANES), F32),
            pltpu.VMEM((EDGE * SUB, LANES), F32),
            pltpu.VMEM((3, (tok + REACH) * SUB, LANES), F32),
            scratch,
            pltpu.VMEM((3, tok * SUB, LANES), F32),
        ],
        compiler_params=params(60),
        cost_estimate=pl.CostEstimate(flops=40_000_000, bytes_accessed=6_000_000, transcendentals=0),
        name="shard",
    )(seq_lengths, fields, *prepared)
    clipped = pl.pallas_call(
        clip_kernel,
        out_shape=jax.ShapeDtypeStruct(weight_grad.shape, F32),
        in_specs=[vmem()] * 2,
        out_specs=vmem(),
        compiler_params=params(60),
        name="clip",
    )(weight_grad, squares)
    return output, stream_grads, clipped


def solution(mesh):
    return jax.shard_map(
        body,
        mesh=mesh,
        in_specs=(
            P(None, "ctx", "ch"),
            P(),
            P(None, None, "ch"),
            P("ch", None),
            P("ch", None),
            P("ctx", "ch"),
        ),
        out_specs=(P("ctx", "ch"), P(None, "ctx", "ch"), P(None, None, "ch")),
        check_vma=False,
    )
```
